32 devices in a mesh: seq: 8 (over z, x), mp: 4 (over y, core).
Axes of the slice: x: 2, y: 2, z: 4, core: 2. Of those that a mesh axis runs over, the one named last changes fastest.
Arguments:
- span_pairs: bfloat16 [4096, 2, 896], P('seq', None, 'mp'), may hold values from -6 to 6
- dec_queries: bfloat16 [4096, 2048], P('seq', 'mp'), may hold values from -6 to 6
- database: float32 [16, 128, 896], P('seq'), may hold values from -6 to 6
- nbr_index: int32 [64, 2], P('seq'), may hold values from 0 to 1
- nbr_host: int32 [64, 2], P('seq'), may hold values from 0 to 7, as said below
- enc_gain: float32 [896], replicated, may hold values from 0.25 to 1.75
- enc_query: bfloat16 [896, 896], P(None, 'mp'), may hold values from -0.1875 to 0.1875
- enc_out: bfloat16 [896, 896], P('mp'), may hold values from -0.1875 to 0.1875
- ffn_gain: float32 [896], replicated, may hold values from 0.25 to 1.75
- ffn_up: bfloat16 [896, 1792], P(None, 'mp'), may hold values from -0.1875 to 0.1875
- ffn_down: bfloat16 [1792, 896], P('mp'), may hold values from -0.125 to 0.125
- dec_kv: bfloat16 [896, 2, 2048], P(None, None, 'mp'), may hold values from -0.1875 to 0.1875
Outputs:
- attended: float32 [4096, 2048], P('seq', 'mp')
The draws below stay inside these ranges and needn't reach their ends.
Inputs may be any that keep to these rules, and one draw needn't show every extreme that they name: `nbr_host`: the 16 neighbours of the spans of one seq index name each host at most 2 times, and some host exactly 2 times. Over all spans every host is named exactly 16 times.
All inputs are finite; a program needn't handle non-finite values.
Results may differ from the reference program's by a relative error of at most 0.019.
Values may be sent and summed in bfloat16 or wider, within the bound.
No kernel may reach another device: no remote copies, remote signals or barrier semaphores. Data moves between devices by JAX's collectives and lax.ppermute only.
A program may use at most 128 MiB of HBM per device.

```python
import jax
import jax.numpy as jnp
from jax import lax

D = 2048
HEADS = 16
HEAD_DIM = 128
E = 896
EHEADS = 8
EHEAD_DIM = 112
FFE = 1792
SPAN = 64
NBL = 128
NEIGH = 2
DB_DEV = 2
CH_DEV = 8
SPANS = 64
TOKENS = 4096
DB_ROWS = 16
N_SEQ = 8
N_MP = 4


def host_table(key):
    inner_key = jax.random.fold_in(key, 17)
    relabel = jax.random.permutation(inner_key, N_SEQ)
    sources = jnp.arange(N_SEQ)[:, None]
    offsets = jnp.arange(NEIGH * CH_DEV)[None, :]
    nominal = (sources + offsets) % N_SEQ
    return relabel[nominal].astype(jnp.int32)


def draw_nbr_host(key, part):
    return host_table(key).reshape(N_SEQ * CH_DEV, NEIGH)


def place_ends(values, key, smallest, high):
    longest = values.shape.index(max(values.shape))
    spots = []
    for shift in (0, 1):
        where = [jax.random.randint(jax.random.fold_in(key, axis), (), 0, length) for axis, length in enumerate(values.shape)]
        where[longest] = (where[longest] + shift) % values.shape[longest]
        spots.append(tuple(where))
    return values.at[spots[0]].set(smallest).at[spots[1]].set(high)


def block_scale(stream_key, shape, pieces, smallest, top_value):
    def one(position, shards_of):
        heights = jax.random.uniform(jax.random.fold_in(jax.random.fold_in(stream_key, 6), position), (shards_of,), jnp.float32, smallest / len(pieces), top_value / len(pieces))
        return jnp.repeat(jnp.exp(heights), shape[position] // shards_of).reshape((-1,) + (1,) * (len(shape) - position - 1))

    level = one(*pieces[0])
    for cut in pieces[1:]:
        level = level * one(*cut)
    return level


def normal_values(key, extent, deviation, limit, shards=(), held_as=jnp.bfloat16):
    array = deviation * jax.random.normal(key, extent, jnp.float32)
    if shards:
        array = array * block_scale(key, extent, shards, -0.22, 0.18)
    return jnp.clip(array, -limit, limit).astype(held_as)


def setup_inputs(seed: int = 0) -> dict:
    arg_keys = jax.random.split(jax.random.key(seed), 13)
    return {
        "span_pairs": normal_values(arg_keys[0], (TOKENS, 2, E), 1.0, 6.0, ((0, 8), (2, 4))),
        "dec_queries": normal_values(arg_keys[1], (TOKENS, D), 1.0, 6.0, ((0, 8), (1, 4))),
        "database": normal_values(arg_keys[2], (DB_ROWS, NBL, E), 1.0, 6.0, ((0, 8),), jnp.float32),
        "nbr_index": place_ends(jax.random.randint(arg_keys[3], (SPANS, NEIGH), 0, DB_DEV), jax.random.fold_in(arg_keys[3], 1), 0, DB_DEV - 1).astype(jnp.int32),
        "nbr_host": draw_nbr_host(jax.random.fold_in(arg_keys[12], 71), 0),
        "enc_gain": jnp.clip(1.0 + 0.15 * jax.random.normal(arg_keys[5], (E,), jnp.float32), 0.25, 1.75),
        "enc_query": normal_values(arg_keys[6], (E, E), E ** -0.5, 0.1875, ((1, 4),)),
        "enc_out": normal_values(arg_keys[7], (E, E), E ** -0.5, 0.1875, ((0, 4),)),
        "ffn_gain": jnp.clip(1.0 + 0.15 * jax.random.normal(arg_keys[8], (E,), jnp.float32), 0.25, 1.75),
        "ffn_up": normal_values(arg_keys[9], (E, FFE), E ** -0.5, 0.1875, ((1, 4),)),
        "ffn_down": normal_values(arg_keys[10], (FFE, E), FFE ** -0.5, 0.125, ((0, 4),)),
        "dec_kv": normal_values(arg_keys[11], (E, 2, D), E ** -0.5, 0.1875, ((2, 4),)),
    }


def rms_scale(values, gain):
    return values * lax.rsqrt(lax.optimization_barrier(jnp.mean(values * values, axis=-1, keepdims=True)) + 1e-06) * gain

def reference(span_pairs, dec_queries, database, nbr_index, nbr_host, enc_gain, enc_query, enc_out, ffn_gain, ffn_up, ffn_down, dec_kv):
    enc_pairs = span_pairs.reshape(SPANS, SPAN, 2, E)
    entries = (nbr_host * DB_DEV + nbr_index).astype(jnp.int32)
    query_blocks = dec_queries.reshape(SPANS, SPAN, D)
    lane_width = E // N_MP
    unit_width = FFE // N_MP
    enc_scale = float(EHEAD_DIM) ** (-0.5)
    dec_scale = float(HEAD_DIM) ** (-0.5)
    out_groups = enc_out.reshape(N_MP, lane_width, E).astype(jnp.float32)
    down_groups = ffn_down.reshape(N_MP, unit_width, E).astype(jnp.float32)
    kv_flat = dec_kv.reshape(E, 2 * D)

    def one_span(inputs):
        rows, pairs, queries_in = inputs
        neighbours = jnp.take(database, rows, axis=0).reshape(NEIGH * NBL, E)
        normed = rms_scale(neighbours, enc_gain).astype(jnp.bfloat16)
        query = (jnp.dot(normed, enc_query, preferred_element_type=jnp.float32) * enc_scale).astype(jnp.bfloat16)
        query = query.reshape(NEIGH * NBL, EHEADS, EHEAD_DIM).astype(jnp.float32)
        keys = pairs[:, 0].reshape(SPAN, EHEADS, EHEAD_DIM).astype(jnp.float32)
        values = pairs[:, 1].reshape(SPAN, EHEADS, EHEAD_DIM).astype(jnp.float32)
        scores = jnp.einsum('rhd,khd->hrk', query, keys)
        weights = jax.nn.softmax(scores, axis=-1).astype(jnp.bfloat16)
        enc_attended = jnp.einsum('hrk,khd->rhd', weights.astype(jnp.float32), values).astype(jnp.bfloat16)
        enc_attended = enc_attended.reshape(NEIGH * NBL, N_MP, lane_width).astype(jnp.float32)
        partial_value = jnp.einsum('rgf,gfe->rge', enc_attended, out_groups).astype(jnp.bfloat16)
        resid = neighbours + lax.optimization_barrier(jnp.sum(partial_value.astype(jnp.float32), axis=1))
        inner = rms_scale(resid, ffn_gain).astype(jnp.bfloat16)
        units = jax.nn.gelu(jnp.dot(inner, ffn_up, preferred_element_type=jnp.float32)).astype(jnp.bfloat16)
        units = units.reshape(NEIGH * NBL, N_MP, unit_width).astype(jnp.float32)
        down_terms = jnp.einsum('rgf,gfe->rge', units, down_groups).astype(jnp.bfloat16)
        encoded = (resid + lax.optimization_barrier(jnp.sum(down_terms.astype(jnp.float32), axis=1))).astype(jnp.bfloat16)
        dec_pairs = jnp.dot(encoded, kv_flat, preferred_element_type=jnp.float32).astype(jnp.bfloat16)
        dec_pairs = dec_pairs.reshape(NEIGH * NBL, 2, HEADS, HEAD_DIM).astype(jnp.float32)
        dec_q = (queries_in.astype(jnp.float32) * dec_scale).astype(jnp.bfloat16)
        dec_q = dec_q.reshape(SPAN, HEADS, HEAD_DIM).astype(jnp.float32)
        dec_scores = jnp.einsum('qhd,khd->hqk', dec_q, dec_pairs[:, 0])
        dec_weights = jax.nn.softmax(dec_scores, axis=-1).astype(jnp.bfloat16)
        result = jnp.einsum('hqk,khd->qhd', dec_weights.astype(jnp.float32), dec_pairs[:, 1])
        return result.reshape(SPAN, D)
    outputs = lax.map(one_span, (entries[:-1], enc_pairs[:-1], query_blocks[1:]))
    first = jnp.zeros((1, SPAN, D), jnp.float32)
    return jnp.concatenate([first, outputs], axis=0).reshape(TOKENS, D)
```

```python
import functools

import jax
import jax.numpy as jnp
from jax import lax
from jax.experimental import pallas as pl
from jax.experimental.pallas import tpu as pltpu
from jax.sharding import PartitionSpec as P

HEAD_DIM = 128
EHEAD_DIM = 112
SPAN = 64
NBL = 128
NEIGH = 2
CH_DEV = 8
HALVES = 2
BLOCK = 512
VMEM_LIMIT = 60 * 1024 * 1024

NT = (((1,), (1,)), ((), ()))
NN = (((1,), (0,)), ((), ()))


def mxu(lhs, rhs, dims):
    return lax.dot_general(lhs, rhs, dims, preferred_element_type=jnp.float32)


def rms_scale(values, gain):
    return values * lax.rsqrt(jnp.mean(values * values, axis=-1, keepdims=True) + 1e-06) * gain


def turned(chunk):
    return jnp.concatenate([chunk[:, SPAN:], chunk[:, :SPAN]], axis=1)


def attention_kernel(lanes, blocks, entries, before, seq_index, gain, *refs):
    refs = list(refs)
    db_refs = [refs.pop(0) for _ in range(blocks)]
    near = [[refs.pop(0) for _ in range(2)] for _ in range(lanes // 2)]
    far = [[refs.pop(0) for _ in range(2)] for _ in range(lanes // 2)]
    kv_refs = [refs.pop(0) for _ in range(lanes)]
    resid, nbrs, weights_in, kv_in, held, nbr_sem, piece_sem, out_sem = refs
    per_host = db_refs[0].shape[0] // 2
    part_rows, width = db_refs[0].shape[1:]
    span_rows = NEIGH * part_rows
    pair_rows = 2 * span_rows
    rows = CH_DEV * span_rows
    pad = HEAD_DIM - EHEAD_DIM
    scale = float(EHEAD_DIM) ** (-0.5)
    here = seq_index[0]
    odd = here % 2
    copies = []
    for span in range(CH_DEV):
        for k in range(NEIGH):
            entry = before[k, 0] if span == 0 else entries[k, span - 1]
            host, index = entry // per_host, entry % per_host
            block = (here // 2 - host // 2 + blocks) % blocks
            place = (here + host) % 2 * per_host + index
            spot = nbrs.at[span * NEIGH + k]
            for b in range(blocks):

                @pl.when(block == b)
                def _(b=b, place=place, spot=spot):
                    pltpu.make_async_copy(db_refs[b].at[place], spot, nbr_sem).start()

            copies.append(pltpu.make_async_copy(db_refs[0].at[0], spot, nbr_sem))
    piece_copies = []
    for p, pair in enumerate(near + far):
        mine = [
            pltpu.make_async_copy(ref, weights_in.at[p, i], piece_sem.at[p, i])
            for i, ref in enumerate(pair)
        ]
        mine.append(pltpu.make_async_copy(kv_refs[p], kv_in.at[p], piece_sem.at[p, 2]))
        for copy in mine:
            copy.start()
        piece_copies.append(mine)
    for copy in copies:
        copy.wait()
    lane = lax.broadcasted_iota(jnp.int32, (pair_rows, 2 * SPAN), 1)
    row = lax.broadcasted_iota(jnp.int32, (pair_rows, 2 * SPAN), 0)
    own_lanes = (lane < SPAN) == (row < span_rows)
    rest = jnp.zeros((pad, 2 * SPAN), jnp.bfloat16)
    empty = jnp.zeros((HEAD_DIM, 2 * SPAN), jnp.bfloat16)
    ones = jnp.ones((2 * HEAD_DIM - EHEAD_DIM, 2 * SPAN), jnp.bfloat16)
    weight_rest = jnp.zeros((pad, width), jnp.bfloat16)
    out_copies = []
    for start in range(0, rows, BLOCK):
        blocks_here = range(start // part_rows, (start + BLOCK) // part_rows)
        values = jnp.concatenate([nbrs[i].astype(jnp.float32) for i in blocks_here], axis=0)
        normed = rms_scale(values, gain[...]).astype(jnp.bfloat16)
        total = values
        for p in range(lanes):
            if start == 0:
                for copy in piece_copies[p]:
                    copy.wait()
            first, second = weights_in[p, 0], weights_in[p, 1]
            if p < lanes // 2:
                q_parts = (first[:EHEAD_DIM], first[EHEAD_DIM:])
                out_parts = (second[:EHEAD_DIM], second[EHEAD_DIM:])
            else:
                first, second = (
                    jnp.where(odd == 0, first, second),
                    jnp.where(odd == 0, second, first),
                )
                q_parts = (first[:EHEAD_DIM], second[:EHEAD_DIM])
                out_parts = (first[EHEAD_DIM:], second[EHEAD_DIM:])
            q_w = jnp.concatenate([q_parts[0], weight_rest, q_parts[1], weight_rest], axis=0)
            out_w = jnp.concatenate([out_parts[0], weight_rest, out_parts[1], weight_rest], axis=0)
            query = (mxu(normed, q_w, NT) * scale).astype(jnp.bfloat16)
            scores = []
            for at in range(0, BLOCK, pair_rows):
                tok = (start + at) // pair_rows * 2 * SPAN
                keys = kv_in[p, 0, :, tok : tok + 2 * SPAN]
                keys = jnp.concatenate(
                    [
                        jnp.concatenate([keys[:EHEAD_DIM], rest, empty], axis=0),
                        jnp.concatenate([empty, turned(keys[EHEAD_DIM:]), rest], axis=0),
                    ],
                    axis=1,
                )
                both = mxu(query[at : at + pair_rows], keys, NN)
                scores.append(jnp.where(own_lanes, both[:, : 2 * SPAN], both[:, 2 * SPAN :]))
            scores = jnp.concatenate(scores, axis=0)
            left = lax.broadcasted_iota(jnp.int32, scores.shape, 1) < SPAN
            low = jnp.max(jnp.where(left, scores, -jnp.inf), axis=1, keepdims=True)
            high = jnp.max(jnp.where(left, -jnp.inf, scores), axis=1, keepdims=True)
            weights = jnp.exp(scores - jnp.where(left, low, high)).astype(jnp.bfloat16)
            attended = []
            for at in range(0, BLOCK, pair_rows):
                tok = (start + at) // pair_rows * 2 * SPAN
                part = weights[at : at + pair_rows]
                vals = kv_in[p, 1, :, tok : tok + 2 * SPAN]
                heads = []
                for head in range(2):
                    picked = jnp.where(own_lanes if head == 0 else ~own_lanes, part, jnp.zeros_like(part))
                    of_head = vals[:EHEAD_DIM] if head == 0 else turned(vals[EHEAD_DIM:])
                    mixed = mxu(picked, jnp.concatenate([of_head, ones], axis=0), NT)
                    heads.append((mixed[:, :HEAD_DIM] / mixed[:, HEAD_DIM:]).astype(jnp.bfloat16))
                attended.append(jnp.concatenate(heads, axis=1))
            total = total + mxu(jnp.concatenate(attended, axis=0), out_w, NN)
        held[start : start + BLOCK, :] = total
        copy = pltpu.make_async_copy(
            held.at[pl.ds(start, BLOCK)], resid.at[pl.ds(start, BLOCK)], out_sem.at[start // BLOCK]
        )
        copy.start()
        out_copies.append(copy)
    for copy in out_copies:
        copy.wait()


def ffn_kernel(near, gain, resid, *refs):
    *group_refs, encoded, resid_in, near_in, far_in, resid_sem, near_sem, far_sem = refs
    count = resid.shape[0] // BLOCK
    resid_copies = [
        pltpu.make_async_copy(
            resid.at[pl.ds(i * BLOCK, BLOCK)], resid_in.at[pl.ds(i * BLOCK, BLOCK)], resid_sem.at[i]
        )
        for i in range(count)
    ]
    resid_copies[0].start()
    copies = []
    for i, ref in enumerate(group_refs):
        if i < 2 * near:
            copies.append(pltpu.make_async_copy(ref, near_in.at[i], near_sem.at[i]))
        else:
            j = i - 2 * near
            copies.append(pltpu.make_async_copy(ref, far_in.at[j], far_sem.at[j]))
        copies[-1].start()
    for copy in resid_copies[1:]:
        copy.start()
    half = far_in.shape[1] // 2
    groups = [([2 * i, 2 * i + 1], near_in.at[2 * i], near_in.at[2 * i + 1]) for i in range(near)]
    for j in range(len(group_refs) - 2 * near):
        groups.append(([2 * near + j], far_in.at[j, pl.ds(0, half)], far_in.at[j, pl.ds(half, half)]))
    for i in range(count):
        resid_copies[i].wait()
        total = resid_in[i * BLOCK : (i + 1) * BLOCK, :]
        normed = rms_scale(total, gain[...]).astype(jnp.bfloat16)

        def raised(g):
            if i == 0:
                for c in groups[g][0]:
                    copies[c].wait()
            return mxu(normed, groups[g][1][...], NT)

        ahead = raised(0)
        for g in range(len(groups)):
            units = ahead
            if g + 1 < len(groups):
                ahead = raised(g + 1)
            total = total + mxu(jax.nn.gelu(units).astype(jnp.bfloat16), groups[g][2][...], NN)
        encoded[i * BLOCK : (i + 1) * BLOCK, :] = total.astype(jnp.bfloat16)


def pairs_kernel(encoded, weights, pairs):
    for start in range(0, encoded.shape[0], BLOCK):
        pairs[start : start + BLOCK, :] = mxu(
            encoded[start : start + BLOCK, :], weights[...], NN
        ).astype(jnp.bfloat16)


def decoder_kernel(first, own_pairs, other, weights, queries, out, other_pairs):
    rows = other.shape[0]
    part = rows // CH_DEV
    width = queries.shape[1]
    scale = float(HEAD_DIM) ** (-0.5)
    for start in range(0, rows, BLOCK):
        other_pairs[start : start + BLOCK, :] = mxu(
            other[start : start + BLOCK, :], weights[...], NN
        ).astype(jnp.bfloat16)

    def span_pairs_of(span, col):
        return jnp.concatenate(
            [r[span * part : (span + 1) * part, col : col + HEAD_DIM] for r in (own_pairs, other_pairs)],
            axis=0,
        )

    for head in range(width // HEAD_DIM):
        col = head * HEAD_DIM
        query = (queries[:, col : col + HEAD_DIM].astype(jnp.float32) * scale).astype(jnp.bfloat16)
        scores = jnp.concatenate(
            [
                mxu(query[span * SPAN : (span + 1) * SPAN], span_pairs_of(span, col), NT)
                for span in range(CH_DEV)
            ],
            axis=0,
        )
        weights_f = jnp.exp(scores - jnp.max(scores, axis=1, keepdims=True))
        weights_f = weights_f / jnp.sum(weights_f, axis=1, keepdims=True)
        weights_b = weights_f.astype(jnp.bfloat16)
        for span in range(CH_DEV):
            result = mxu(
                weights_b[span * SPAN : (span + 1) * SPAN], span_pairs_of(span, width + col), NN
            )
            if span == 0:
                result = jnp.where(first[0] == 0, jnp.zeros_like(result), result)
            out[span * SPAN : (span + 1) * SPAN, col : col + HEAD_DIM] = result


def call(body, out_shape, in_specs, name, flops, scratch=(), out="v"):
    spaces = {"s": pltpu.SMEM, "v": pltpu.VMEM, "h": pl.ANY}
    return pl.pallas_call(
        body,
        out_shape=out_shape,
        in_specs=[pl.BlockSpec(memory_space=spaces[c]) for c in in_specs],
        out_specs=pl.BlockSpec(memory_space=spaces[out]),
        scratch_shapes=list(scratch),
        compiler_params=pltpu.CompilerParams(vmem_limit_bytes=VMEM_LIMIT),
        cost_estimate=pl.CostEstimate(flops=flops, bytes_accessed=8_000_000, transcendentals=0),
        name=name,
    )


def on_device(
    span_pairs,
    dec_queries,
    database,
    nbr_index,
    nbr_host,
    enc_gain,
    enc_query,
    enc_out,
    ffn_gain,
    ffn_up,
    ffn_down,
    dec_kv,
):
    seq_size = lax.axis_size("seq")
    lanes = lax.axis_size("mp")
    seq_index = lax.axis_index("seq")
    lane_index = lax.axis_index("mp")
    entries_here, block_rows, width = database.shape
    half_rows = block_rows // HALVES
    rows = CH_DEV * NEIGH * half_rows
    blocks = seq_size // 2
    odd = seq_index % 2
    far_lanes = lanes // 2 - 1

    def core_swap(array):
        return lax.ppermute(array, "mp", [(i, i ^ 1) for i in range(lanes)])

    def lane_step(array, step):
        return lax.ppermute(array, "mp", [(i, (i + 2 * step) % lanes) for i in range(lanes)])

    def seq_swap(array):
        return lax.ppermute(array, "seq", [(i, i ^ 1) for i in range(seq_size)])

    def seq_ring(array):
        return lax.ppermute(array, "seq", [(i, (i + 2) % seq_size) for i in range(seq_size)])

    def next_seq(array):
        return lax.ppermute(array, "seq", [(i, i + 1) for i in range(seq_size - 1)])

    def half_of(arrays):
        return jnp.concatenate(
            [
                lax.dynamic_slice_in_dim(a, odd * (a.shape[0] // 2), a.shape[0] // 2, 0)
                for a in arrays
            ],
            axis=0,
        )

    def after(array, *others):
        return lax.optimization_barrier((array, *others))[0]

    query_t, up_t = enc_query.T, ffn_up.T
    kv_t = jnp.transpose(span_pairs, (1, 2, 0))
    kv_rows, tokens = kv_t.shape[1:]
    kept = tokens - SPAN

    entries = (nbr_host * entries_here + nbr_index).T
    digits = jnp.stack([entries[:, CH_DEV - 1] // 128, entries[:, CH_DEV - 1] % 128], axis=1)
    digits = jnp.broadcast_to(digits[:, :, None], (2, 2, SPAN)).astype(jnp.bfloat16)
    packet = jnp.concatenate([kv_t[:, :, kept:], jnp.pad(digits, ((0, 0), (0, 14), (0, 0)))], axis=1)

    attention_half = half_of((query_t, enc_out))
    attention_far = [lane_step(attention_half, n + 1) for n in range(far_lanes)]
    packet = next_seq(packet)
    database_half = lax.dynamic_slice_in_dim(
        database, (lane_index % HALVES) * half_rows, half_rows, 1
    ).astype(jnp.bfloat16)
    block = jnp.concatenate([database_half, seq_swap(database_half)], axis=0)
    attention_core = (core_swap(query_t), core_swap(enc_out))

    database_blocks = [block]
    for _ in range(blocks - 1):
        database_blocks.append(seq_ring(database_blocks[-1]))

    before = packet[:, kv_rows : kv_rows + 2, 0].astype(jnp.int32)
    before = before[:, :1] * 128 + before[:, 1:]
    kv_t = jnp.concatenate([packet[:, :kv_rows], kv_t[:, :, :kept]], axis=2)

    ffn_half = after(half_of((up_t, ffn_down)), *attention_far)
    ffn_far = [lane_step(ffn_half, n + 1) for n in range(far_lanes)]
    attention_cross = [seq_swap(a) for a in attention_far]
    kv_core = core_swap(kv_t)
    kv_send = after(kv_t, *ffn_far)
    kv_far = [lane_step(kv_send, n + 1) for n in range(far_lanes)]
    ffn_cross = [seq_swap(a) for a in ffn_far]
    up_send, down_send = after((up_t, ffn_down), *attention_cross)
    ffn_core = (core_swap(up_send), core_swap(down_send))

    kv_pieces = [kv_t, kv_core]
    attention_pieces = [query_t, enc_out, *attention_core]
    for straight, crossed, kv in zip(attention_far, attention_cross, kv_far):
        attention_pieces += [straight, crossed, core_swap(straight), core_swap(crossed)]
        kv_pieces += [kv, core_swap(kv)]
    ffn_pieces = [up_t, ffn_down, *ffn_core]
    for piece in ffn_far + ffn_cross:
        ffn_pieces += [piece, core_swap(piece)]

    gemm = 2 * rows * width * width
    here = seq_index.reshape(1).astype(jnp.int32)
    spans_in = CH_DEV * NEIGH
    steps = rows // BLOCK
    dma = pltpu.SemaphoreType.DMA
    resid = call(
        functools.partial(attention_kernel, lanes, blocks),
        jax.ShapeDtypeStruct((rows, width), jnp.float32),
        "sss" + "v" + "h" * (blocks + 3 * lanes),
        "encoder_attention",
        2 * gemm,
        scratch=[
            pltpu.VMEM((spans_in, half_rows, width), jnp.bfloat16),
            pltpu.VMEM((lanes, 2, *enc_out.shape), jnp.bfloat16),
            pltpu.VMEM((lanes, *kv_t.shape), jnp.bfloat16),
            pltpu.VMEM((rows, width), jnp.float32),
            dma,
            dma((lanes, 3)),
            dma((steps,)),
        ],
        out="h",
    )(
        entries,
        before,
        here,
        enc_gain.reshape(1, width),
        *database_blocks,
        *attention_pieces,
        *kv_pieces,
    )
    far_pieces = len(ffn_pieces) - 4
    encoded = call(
        functools.partial(ffn_kernel, 2),
        jax.ShapeDtypeStruct((rows, width), jnp.bfloat16),
        "v" + "h" * (1 + len(ffn_pieces)),
        "encoder_ffn",
        4 * gemm,
        scratch=[
            pltpu.VMEM((rows, width), jnp.float32),
            pltpu.VMEM((4, *ffn_down.shape), jnp.bfloat16),
            pltpu.VMEM((far_pieces, *ffn_down.shape), jnp.bfloat16),
            dma((steps,)),
            dma((4,)),
            dma((far_pieces,)),
        ],
    )(ffn_gain.reshape(1, width), resid, *ffn_pieces)

    other = core_swap(encoded)
    dec_width = dec_kv.shape[2]
    kv_weights = dec_kv.reshape(width, 2 * dec_width)
    pairs_shape = (rows, 2 * dec_width)
    pairs_flops = 2 * rows * width * 2 * dec_width
    own_pairs = call(
        pairs_kernel, jax.ShapeDtypeStruct(pairs_shape, jnp.bfloat16), "vv", "decoder_pairs", pairs_flops
    )(encoded, kv_weights)
    return call(
        decoder_kernel,
        jax.ShapeDtypeStruct(dec_queries.shape, jnp.float32),
        "svvvv",
        "decoder_attention",
        pairs_flops,
        scratch=[pltpu.VMEM(pairs_shape, jnp.bfloat16)],
    )(here, own_pairs, other, kv_weights, dec_queries)


def solution(mesh):
    placed = (
        P("seq", None, "mp"),
        P("seq", "mp"),
        P("seq", None, None),
        P("seq", None),
        P("seq", None),
        P(),
        P(None, "mp"),
        P("mp", None),
        P(),
        P(None, "mp"),
        P("mp", None),
        P(None, None, "mp"),
    )
    return jax.shard_map(
        on_device, mesh=mesh, in_specs=placed, out_specs=P("seq", "mp"), check_vma=False
    )
```

```python
import functools

import jax
import jax.numpy as jnp
from jax import lax
from jax.experimental import pallas as pl
from jax.experimental.pallas import tpu as pltpu
from jax.sharding import PartitionSpec as P

HEAD_DIM = 128
EHEAD_DIM = 112
SPAN = 64
NBL = 128
NEIGH = 2
CH_DEV = 8
HALVES = 2
BLOCK = 512
DIGIT = 128

NT = (((1,), (1,)), ((), ()))
NN = (((1,), (0,)), ((), ()))


def mxu(lhs, rhs, dims):
    return lax.dot_general(lhs, rhs, dims, preferred_element_type=jnp.float32)


def rms_scale(values, gain):
    return values * lax.rsqrt(jnp.mean(values * values, axis=-1, keepdims=True) + 1e-06) * gain


def turned(chunk):
    return jnp.concatenate([chunk[:, SPAN:], chunk[:, :SPAN]], axis=1)


def prepare_kernel(place, host, index, database, query_t, enc_out, up_t, down, kv_t, *refs):
    db_half, attention_half, ffn_half, packet, db_in, kv_in, sems = refs
    per_host, half_rows, width = db_half.shape
    seq, lane = place[0], place[1]
    copies = [
        pltpu.make_async_copy(
            database.at[:, pl.ds(pl.multiple_of(lane % HALVES * half_rows, half_rows), half_rows)],
            db_in,
            sems.at[0],
        ),
        pltpu.make_async_copy(kv_t.at[:, :, pl.ds(kv_t.shape[2] - 2 * SPAN, 2 * SPAN)], kv_in, sems.at[1]),
    ]
    halves = ((query_t, attention_half, 0, seq % 2), (enc_out, attention_half, 1, seq % 2))
    halves += ((up_t, ffn_half, 0, seq // 2 % 2), (down, ffn_half, 1, seq // 2 % 2))
    for i, (source, target, spot, parity) in enumerate(halves):
        count = source.shape[0] // 2
        copies.append(
            pltpu.make_async_copy(
                source.at[pl.ds(pl.multiple_of(parity * count, 16), count)],
                target.at[pl.ds(spot * count, count)],
                sems.at[2 + i],
            )
        )
    for copy in copies:
        copy.start()
    copies[0].wait()
    db_half[...] = db_in[...].astype(jnp.bfloat16)
    copies[1].wait()
    kv_rows = kv_in.shape[1]
    row = lax.broadcasted_iota(jnp.int32, (packet.shape[1] - kv_rows, SPAN), 0)
    for k in range(NEIGH):
        entry = host[k, CH_DEV - 1] * per_host + index[k, CH_DEV - 1]
        digits = jnp.where(row == 0, entry // DIGIT, jnp.where(row == 1, entry % DIGIT, 0))
        packet[k, :kv_rows, :] = kv_in[k][:, SPAN:]
        packet[k, kv_rows:, :] = digits.astype(jnp.float32).astype(jnp.bfloat16)
    for copy in copies[2:]:
        copy.wait()


def gather_kernel(blocks, here, host, index, before, gain, *refs):
    *db_refs, values_out, normed_out, nbrs, sems = refs
    per_host, part_rows, width = db_refs[0].shape
    seq = here[0]
    copies = []
    for i in range(nbrs.shape[0]):
        span, k = i // NEIGH, i % NEIGH
        if span == 0:
            of_host, place = before[k, 0] // per_host, before[k, 0] % per_host
        else:
            of_host, place = host[k, span - 1], index[k, span - 1]
        block = (seq // 2 - of_host // 2 + blocks) % blocks * 2 + (seq + of_host) % 2
        for b in range(2 * blocks):

            @pl.when(block == b)
            def _(b=b, place=place, i=i):
                pltpu.make_async_copy(db_refs[b].at[place], nbrs.at[i], sems.at[i]).start()

        copies.append(pltpu.make_async_copy(db_refs[0].at[0], nbrs.at[i], sems.at[i]))
    for i in range(nbrs.shape[0]):
        copies[i].wait()
        values = nbrs[i].astype(jnp.float32)
        at = slice(i * part_rows, (i + 1) * part_rows)
        values_out[at, :] = values
        normed_out[at, :] = rms_scale(values, gain[...]).astype(jnp.bfloat16)


def attention_kernel(pieces, far, seq_index, before, normed_in, *refs):
    weight_refs, kv_refs, (result,) = refs[: 2 * pieces], refs[2 * pieces : 3 * pieces], refs[3 * pieces :]
    rows, width = before.shape
    span_rows = rows // CH_DEV
    pair_rows = 2 * span_rows
    pad = HEAD_DIM - EHEAD_DIM
    scale = float(EHEAD_DIM) ** (-0.5)
    odd = seq_index[0] % 2
    lane = lax.broadcasted_iota(jnp.int32, (pair_rows, 2 * SPAN), 1)
    row = lax.broadcasted_iota(jnp.int32, (pair_rows, 2 * SPAN), 0)
    own_lanes = (lane < SPAN) == (row < span_rows)
    rest = jnp.zeros((pad, 2 * SPAN), jnp.bfloat16)
    empty = jnp.zeros((HEAD_DIM, 2 * SPAN), jnp.bfloat16)
    ones = jnp.ones((2 * HEAD_DIM - EHEAD_DIM, 2 * SPAN), jnp.bfloat16)
    weight_rest = jnp.zeros((pad, width), jnp.bfloat16)
    for p in range(pieces):
        first, second = weight_refs[2 * p][...], weight_refs[2 * p + 1][...]
        if far:
            first, second = (
                jnp.where(odd == 0, first, second),
                jnp.where(odd == 0, second, first),
            )
            q_parts = (first[:EHEAD_DIM], second[:EHEAD_DIM])
            out_parts = (first[EHEAD_DIM:], second[EHEAD_DIM:])
        else:
            q_parts = (first[:EHEAD_DIM], first[EHEAD_DIM:])
            out_parts = (second[:EHEAD_DIM], second[EHEAD_DIM:])
        q_w = jnp.concatenate([q_parts[0], weight_rest, q_parts[1], weight_rest], axis=0)
        out_w = jnp.concatenate([out_parts[0], weight_rest, out_parts[1], weight_rest], axis=0)
        for start in range(0, rows, BLOCK):
            block = slice(start, start + BLOCK)
            query = (mxu(normed_in[block, :], q_w, NT) * scale).astype(jnp.bfloat16)
            scores = []
            for at in range(0, BLOCK, pair_rows):
                tok = (start + at) // pair_rows * 2 * SPAN
                keys = kv_refs[p][0, :, tok : tok + 2 * SPAN]
                keys = jnp.concatenate(
                    [
                        jnp.concatenate([keys[:EHEAD_DIM], rest, empty], axis=0),
                        jnp.concatenate([empty, turned(keys[EHEAD_DIM:]), rest], axis=0),
                    ],
                    axis=1,
                )
                both = mxu(query[at : at + pair_rows], keys, NN)
                scores.append(jnp.where(own_lanes, both[:, : 2 * SPAN], both[:, 2 * SPAN :]))
            scores = jnp.concatenate(scores, axis=0)
            left = lax.broadcasted_iota(jnp.int32, scores.shape, 1) < SPAN
            low = jnp.max(jnp.where(left, scores, -jnp.inf), axis=1, keepdims=True)
            high = jnp.max(jnp.where(left, -jnp.inf, scores), axis=1, keepdims=True)
            weights = jnp.exp(scores - jnp.where(left, low, high)).astype(jnp.bfloat16)
            attended = []
            for at in range(0, BLOCK, pair_rows):
                tok = (start + at) // pair_rows * 2 * SPAN
                part = weights[at : at + pair_rows]
                vals = kv_refs[p][1, :, tok : tok + 2 * SPAN]
                heads = []
                for head in range(2):
                    picked = jnp.where(own_lanes if head == 0 else ~own_lanes, part, jnp.zeros_like(part))
                    of_head = vals[:EHEAD_DIM] if head == 0 else turned(vals[EHEAD_DIM:])
                    mixed = mxu(picked, jnp.concatenate([of_head, ones], axis=0), NT)
                    heads.append((mixed[:, :HEAD_DIM] / mixed[:, HEAD_DIM:]).astype(jnp.bfloat16))
                attended.append(jnp.concatenate(heads, axis=1))
            so_far = before if p == 0 else result
            result[block, :] = so_far[block, :] + mxu(jnp.concatenate(attended, axis=0), out_w, NN)


def ffn_kernel(far, first, gain, before, *refs):
    if first:
        *group_refs, total, normed = refs
        normed[...] = rms_scale(before[...], gain[...]).astype(jnp.bfloat16)
        result = total
    else:
        normed, *group_refs, result, total = refs
    if far:
        half = group_refs[0].shape[0] // 2
        groups = [(r.at[pl.ds(0, half)], r.at[pl.ds(half, half)]) for r in group_refs]
    else:
        groups = list(zip(group_refs[::2], group_refs[1::2]))
    ahead = mxu(normed[...], groups[0][0][...], NT)
    for g in range(len(groups)):
        units = ahead
        if g + 1 < len(groups):
            ahead = mxu(normed[...], groups[g + 1][0][...], NT)
        added = mxu(jax.nn.gelu(units).astype(jnp.bfloat16), groups[g][1][...], NN)
        added = (before if g == 0 else total)[...] + added
        if g + 1 < len(groups):
            total[...] = added
        else:
            result[...] = added.astype(result.dtype)


def pairs_kernel(encoded, weights, pairs):
    pairs[...] = mxu(encoded[...], weights[...], NN).astype(jnp.bfloat16)


def decoder_kernel(first, own_pairs, other, weights, queries, out, other_pairs):
    rows = other.shape[0]
    part = rows // CH_DEV
    width = queries.shape[1]
    scale = float(HEAD_DIM) ** (-0.5)
    other_pairs[...] = mxu(other[...], weights[...], NN).astype(jnp.bfloat16)

    def span_pairs_of(span, col):
        return jnp.concatenate(
            [r[span * part : (span + 1) * part, col : col + HEAD_DIM] for r in (own_pairs, other_pairs)],
            axis=0,
        )

    for head in range(width // HEAD_DIM):
        col = head * HEAD_DIM
        query = (queries[:, col : col + HEAD_DIM].astype(jnp.float32) * scale).astype(jnp.bfloat16)
        scores = jnp.concatenate(
            [
                mxu(query[span * SPAN : (span + 1) * SPAN], span_pairs_of(span, col), NT)
                for span in range(CH_DEV)
            ],
            axis=0,
        )
        weights_f = jnp.exp(scores - jnp.max(scores, axis=1, keepdims=True))
        weights_f = weights_f / jnp.sum(weights_f, axis=1, keepdims=True)
        weights_b = weights_f.astype(jnp.bfloat16)
        for span in range(CH_DEV):
            result = mxu(
                weights_b[span * SPAN : (span + 1) * SPAN], span_pairs_of(span, width + col), NN
            )
            if span == 0:
                result = jnp.where(first[0] == 0, jnp.zeros_like(result), result)
            out[span * SPAN : (span + 1) * SPAN, col : col + HEAD_DIM] = result


def call(body, out_shape, in_specs, name, flops, vmem_mib, scratch=()):
    spaces = {"s": pltpu.SMEM, "v": pltpu.VMEM, "h": pl.ANY}
    return pl.pallas_call(
        body,
        out_shape=out_shape,
        in_specs=[pl.BlockSpec(memory_space=spaces[c]) for c in in_specs],
        out_specs=jax.tree.map(lambda _: pl.BlockSpec(memory_space=pltpu.VMEM), out_shape),
        scratch_shapes=list(scratch),
        compiler_params=pltpu.CompilerParams(vmem_limit_bytes=vmem_mib * 1024 * 1024),
        cost_estimate=pl.CostEstimate(flops=flops, bytes_accessed=8_000_000, transcendentals=0),
        name=name,
    )


def on_device(
    span_pairs,
    dec_queries,
    database,
    nbr_index,
    nbr_host,
    enc_gain,
    enc_query,
    enc_out,
    ffn_gain,
    ffn_up,
    ffn_down,
    dec_kv,
):
    seq_size = lax.axis_size("seq")
    lanes = lax.axis_size("mp")
    seq_index = lax.axis_index("seq")
    lane_index = lax.axis_index("mp")
    entries_here, block_rows, width = database.shape
    half_rows = block_rows // HALVES
    rows = CH_DEV * NEIGH * half_rows
    blocks = seq_size // 2
    far_lanes = lanes // 2 - 1

    def core_swap(array):
        return lax.ppermute(array, "mp", [(i, i ^ 1) for i in range(lanes)])

    def lane_step(array, step):
        return lax.ppermute(array, "mp", [(i, (i + 2 * step) % lanes) for i in range(lanes)])

    def seq_swap(array):
        return lax.ppermute(array, "seq", [(i, i ^ 1) for i in range(seq_size)])

    def seq_cross(array):
        return lax.ppermute(array, "seq", [(i, i ^ 2) for i in range(seq_size)])

    def seq_ring(array):
        return lax.ppermute(array, "seq", [(i, (i + 2) % seq_size) for i in range(seq_size)])

    def next_seq(array):
        return lax.ppermute(array, "seq", [(i, i + 1) for i in range(seq_size - 1)])

    def after(array, *others):
        return lax.optimization_barrier((array, *others))[0]

    query_t, up_t = enc_query.T, ffn_up.T
    kv_t = jnp.transpose(span_pairs, (1, 2, 0))
    kv_rows, tokens = kv_t.shape[1:]
    kept = tokens - SPAN

    here = seq_index.reshape(1).astype(jnp.int32)
    place = jnp.stack([seq_index, lane_index]).astype(jnp.int32)
    host, index = nbr_host.T, nbr_index.T
    dma = pltpu.SemaphoreType.DMA
    short = functools.partial(jax.ShapeDtypeStruct, dtype=jnp.bfloat16)
    database_half, attention_half, ffn_half, packet = call(
        prepare_kernel,
        (
            short((entries_here, half_rows, width)),
            short(enc_out.shape),
            short(ffn_down.shape),
            short((2, kv_rows + 16, SPAN)),
        ),
        "sss" + "h" * 6,
        "prepare",
        rows * width,
        8,
        scratch=[
            pltpu.VMEM((entries_here, half_rows, width), jnp.float32),
            pltpu.VMEM((2, kv_rows, 2 * SPAN), jnp.bfloat16),
            dma((6,)),
        ],
    )(place, host, index, database, query_t, enc_out, up_t, ffn_down, kv_t)

    attention_far = [lane_step(attention_half, n + 1) for n in range(far_lanes)]
    packet = next_seq(packet)
    database_ring = [database_half]
    for _ in range(blocks - 1):
        database_ring.append(seq_ring(database_ring[-1]))
    database_blocks = []
    for block in database_ring:
        database_blocks += [block, seq_swap(block)]

    dec_width = dec_kv.shape[2]
    kv_weights = dec_kv.reshape(width, 2 * dec_width)
    enc_gain, ffn_gain = enc_gain.reshape(1, width), ffn_gain.reshape(1, width)
    before = packet[:, kv_rows : kv_rows + 2, 0].astype(jnp.int32)
    before = before[:, :1] * DIGIT + before[:, 1:]
    kv_t = jnp.concatenate([packet[:, :kv_rows], kv_t[:, :, :kept]], axis=2)

    near_step = database_ring[min(1, blocks - 1)]
    ffn_far = [
        lane_step(after(ffn_half, packet, near_step, database_blocks[1], *attention_far), n + 1)
        for n in range(far_lanes)
    ]
    attention_core = tuple(core_swap(a) for a in after((query_t, enc_out), database_ring[-1]))
    attention_cross = [seq_swap(after(a, *database_blocks)) for a in attention_far]
    kv_t, kv_weights, enc_gain, ffn_gain, before, *_ = lax.optimization_barrier(
        (kv_t, kv_weights, enc_gain, ffn_gain, before, database_blocks[min(3, 2 * blocks - 1)])
    )
    kv_core = core_swap(kv_t)
    kv_send = after(kv_t, *ffn_far, *database_blocks)
    kv_far = [lane_step(kv_send, n + 1) for n in range(far_lanes)]
    ffn_cross = [seq_cross(a) for a in ffn_far]
    up_send, down_send = after((up_t, ffn_down), *attention_cross)
    ffn_core = (core_swap(up_send), core_swap(down_send))

    gemm = 2 * rows * width * width
    long_rows = jax.ShapeDtypeStruct((rows, width), jnp.float32)
    short_rows = short((rows, width))
    values, normed = call(
        functools.partial(gather_kernel, blocks),
        (long_rows, short_rows),
        "ssssv" + "h" * 2 * blocks,
        "neighbour_rows",
        10 * rows * width,
        16,
        scratch=[
            pltpu.VMEM((CH_DEV * NEIGH, half_rows, width), jnp.bfloat16),
            dma((CH_DEV * NEIGH,)),
        ],
    )(here, host, index, before, enc_gain, *database_blocks)

    def attention(so_far, weights, kv, far):
        return call(
            functools.partial(attention_kernel, len(kv), far),
            long_rows,
            "svv" + "v" * 3 * len(kv),
            "encoder_attention",
            gemm * 2 * len(kv) // lanes,
            24,
        )(here, so_far, normed, *weights, *kv)

    partial_rows = attention(values, (query_t, enc_out, *attention_core), (kv_t, kv_core), False)
    far_weights, far_kv = [], []
    kv_forward = after(tuple(kv_far), partial_rows)
    for straight, crossed, kv, forward in zip(attention_far, attention_cross, kv_far, kv_forward):
        far_weights += [straight, crossed, core_swap(straight), core_swap(crossed)]
        far_kv += [kv, core_swap(forward)]
    resid = attention(partial_rows, far_weights, far_kv, True)

    near_units = (up_t, ffn_down, *ffn_core)
    partial_rows, normed = call(
        functools.partial(ffn_kernel, False, True),
        (long_rows, short_rows),
        "vv" + "v" * len(near_units),
        "encoder_ffn_near",
        2 * gemm,
        30,
    )(ffn_gain, resid, *near_units)
    ffn_cross = after(tuple(ffn_cross), resid)
    far_units = [p for piece in [*ffn_far, *ffn_cross] for p in (piece, core_swap(piece))]
    encoded = call(
        functools.partial(ffn_kernel, True, False),
        short_rows,
        "vvv" + "v" * len(far_units),
        "encoder_ffn_far",
        2 * gemm,
        30,
        scratch=[pltpu.VMEM((rows, width), jnp.float32)],
    )(ffn_gain, partial_rows, normed, *far_units)

    other = core_swap(encoded)
    pairs_shape = (rows, 2 * dec_width)
    pairs_flops = 2 * rows * width * 2 * dec_width
    own_pairs = call(
        pairs_kernel,
        jax.ShapeDtypeStruct(pairs_shape, jnp.bfloat16),
        "vv",
        "decoder_pairs",
        pairs_flops,
        20,
    )(encoded, kv_weights)
    return call(
        decoder_kernel,
        jax.ShapeDtypeStruct(dec_queries.shape, jnp.float32),
        "svvvv",
        "decoder_attention",
        pairs_flops,
        28,
        scratch=[pltpu.VMEM(pairs_shape, jnp.bfloat16)],
    )(here, own_pairs, other, kv_weights, dec_queries)


def solution(mesh):
    placed = (
        P("seq", None, "mp"),
        P("seq", "mp"),
        P("seq", None, None),
        P("seq", None),
        P("seq", None),
        P(),
        P(None, "mp"),
        P("mp", None),
        P(),
        P(None, "mp"),
        P("mp", None),
        P(None, None, "mp"),
    )
    return jax.shard_map(
        on_device, mesh=mesh, in_specs=placed, out_specs=P("seq", "mp"), check_vma=False
    )
```

```python
import functools

import jax
import jax.numpy as jnp
from jax import lax
from jax.experimental import pallas as pl
from jax.experimental.pallas import tpu as pltpu
from jax.sharding import PartitionSpec as P

HEAD_DIM = 128
EHEAD_DIM = 112
SPAN = 64
NBL = 128
NEIGH = 2
CH_DEV = 8
HALVES = 2
BLOCK = 512
DIGIT = 128

NT = (((1,), (1,)), ((), ()))
NN = (((1,), (0,)), ((), ()))


def mxu(lhs, rhs, dims):
    return lax.dot_general(lhs, rhs, dims, preferred_element_type=jnp.float32)


def rms_scale(values, gain):
    return values * lax.rsqrt(jnp.mean(values * values, axis=-1, keepdims=True) + 1e-06) * gain


def turned(chunk):
    return jnp.concatenate([chunk[:, SPAN:], chunk[:, :SPAN]], axis=1)


def prepare_kernel(here, lane_here, host, index, database, query_t, enc_out, up_t, down, kv_t, *refs):
    db_half, attention_half, ffn_half, packet, db_in, kv_in, sems = refs
    per_host, half_rows, width = db_half.shape
    seq, lane = here[0], lane_here[0]
    copies = [
        pltpu.make_async_copy(
            database.at[:, pl.ds(pl.multiple_of(lane % HALVES * half_rows, half_rows), half_rows)],
            db_in,
            sems.at[0],
        ),
        pltpu.make_async_copy(kv_t.at[:, :, pl.ds(kv_t.shape[2] - 2 * SPAN, 2 * SPAN)], kv_in, sems.at[1]),
    ]
    halves = ((query_t, attention_half, 0, seq % 2), (enc_out, attention_half, 1, seq % 2))
    halves += ((up_t, ffn_half, 0, seq // 2 % 2), (down, ffn_half, 1, seq // 2 % 2))
    for i, (source, target, spot, parity) in enumerate(halves):
        count = source.shape[0] // 2
        copies.append(
            pltpu.make_async_copy(
                source.at[pl.ds(pl.multiple_of(parity * count, 16), count)],
                target.at[pl.ds(spot * count, count)],
                sems.at[2 + i],
            )
        )
    for copy in copies:
        copy.start()
    copies[0].wait()
    db_half[...] = db_in[...].astype(jnp.bfloat16)
    copies[1].wait()
    kv_rows = kv_in.shape[1]
    row = lax.broadcasted_iota(jnp.int32, (packet.shape[1] - kv_rows, SPAN), 0)
    for k in range(NEIGH):
        entry = host[k, CH_DEV - 1] * per_host + index[k, CH_DEV - 1]
        digits = jnp.where(row == 0, entry // DIGIT, jnp.where(row == 1, entry % DIGIT, 0))
        packet[k, :kv_rows, :] = kv_in[k][:, SPAN:]
        packet[k, kv_rows:, :] = digits.astype(jnp.float32).astype(jnp.bfloat16)
    for copy in copies[2:]:
        copy.wait()


def gather_kernel(blocks, here, host, index, before, gain, *refs):
    *db_refs, rows_out, normed_out = refs
    per_host, part_rows, width = db_refs[0].shape
    seq = here[0]
    for i in range(CH_DEV * NEIGH):
        span, k = i // NEIGH, i % NEIGH
        if span == 0:
            of_host, place = before[k, 0] // per_host, before[k, 0] % per_host
        else:
            of_host, place = host[k, span - 1], index[k, span - 1]
        block = (seq // 2 - of_host // 2 + blocks) % blocks * 2 + (seq + of_host) % 2
        for b in range(2 * blocks):

            @pl.when(block == b)
            def _(b=b, place=place, i=i):
                rows_out[i * part_rows : (i + 1) * part_rows, :] = db_refs[b][place]

    values = rows_out[...].astype(jnp.float32)
    normed_out[...] = rms_scale(values, gain[...]).astype(jnp.bfloat16)


def attention_kernel(pieces, far, seq_index, before, normed_in, *refs):
    weight_refs, kv_refs, (result,) = refs[: 2 * pieces], refs[2 * pieces : 3 * pieces], refs[3 * pieces :]
    rows, width = before.shape
    span_rows = rows // CH_DEV
    pair_rows = 2 * span_rows
    pad = HEAD_DIM - EHEAD_DIM
    scale = float(EHEAD_DIM) ** (-0.5)
    odd = seq_index[0] % 2
    lane = lax.broadcasted_iota(jnp.int32, (pair_rows, 2 * SPAN), 1)
    row = lax.broadcasted_iota(jnp.int32, (pair_rows, 2 * SPAN), 0)
    own_lanes = (lane < SPAN) == (row < span_rows)
    rest = jnp.zeros((pad, 2 * SPAN), jnp.bfloat16)
    empty = jnp.zeros((HEAD_DIM, 2 * SPAN), jnp.bfloat16)
    ones = jnp.ones((2 * HEAD_DIM - EHEAD_DIM, 2 * SPAN), jnp.bfloat16)
    weight_rest = jnp.zeros((pad, width), jnp.bfloat16)
    for p in range(pieces):
        first, second = weight_refs[2 * p][...], weight_refs[2 * p + 1][...]
        if far:
            first, second = (
                jnp.where(odd == 0, first, second),
                jnp.where(odd == 0, second, first),
            )
            q_parts = (first[:EHEAD_DIM], second[:EHEAD_DIM])
            out_parts = (first[EHEAD_DIM:], second[EHEAD_DIM:])
        else:
            q_parts = (first[:EHEAD_DIM], first[EHEAD_DIM:])
            out_parts = (second[:EHEAD_DIM], second[EHEAD_DIM:])
        q_w = jnp.concatenate([q_parts[0], weight_rest, q_parts[1], weight_rest], axis=0)
        out_w = jnp.concatenate([out_parts[0], weight_rest, out_parts[1], weight_rest], axis=0)
        for start in range(0, rows, BLOCK):
            block = slice(start, start + BLOCK)
            query = (mxu(normed_in[block, :], q_w, NT) * scale).astype(jnp.bfloat16)
            scores = []
            for at in range(0, BLOCK, pair_rows):
                tok = (start + at) // pair_rows * 2 * SPAN
                keys = kv_refs[p][0, :, tok : tok + 2 * SPAN]
                keys = jnp.concatenate(
                    [
                        jnp.concatenate([keys[:EHEAD_DIM], rest, empty], axis=0),
                        jnp.concatenate([empty, turned(keys[EHEAD_DIM:]), rest], axis=0),
                    ],
                    axis=1,
                )
                both = mxu(query[at : at + pair_rows], keys, NN)
                scores.append(jnp.where(own_lanes, both[:, : 2 * SPAN], both[:, 2 * SPAN :]))
            scores = jnp.concatenate(scores, axis=0)
            left = lax.broadcasted_iota(jnp.int32, scores.shape, 1) < SPAN
            low = jnp.max(jnp.where(left, scores, -jnp.inf), axis=1, keepdims=True)
            high = jnp.max(jnp.where(left, -jnp.inf, scores), axis=1, keepdims=True)
            weights = jnp.exp(scores - jnp.where(left, low, high)).astype(jnp.bfloat16)
            attended = []
            for at in range(0, BLOCK, pair_rows):
                tok = (start + at) // pair_rows * 2 * SPAN
                part = weights[at : at + pair_rows]
                vals = kv_refs[p][1, :, tok : tok + 2 * SPAN]
                heads = []
                for head in range(2):
                    picked = jnp.where(own_lanes if head == 0 else ~own_lanes, part, jnp.zeros_like(part))
                    of_head = vals[:EHEAD_DIM] if head == 0 else turned(vals[EHEAD_DIM:])
                    mixed = mxu(picked, jnp.concatenate([of_head, ones], axis=0), NT)
                    heads.append((mixed[:, :HEAD_DIM] / mixed[:, HEAD_DIM:]).astype(jnp.bfloat16))
                attended.append(jnp.concatenate(heads, axis=1))
            so_far = before if p == 0 else result
            result[block, :] = so_far[block, :].astype(jnp.float32) + mxu(jnp.concatenate(attended, axis=0), out_w, NN)


def ffn_kernel(far, first, gain, before, *refs):
    if first:
        *group_refs, total, normed = refs
        normed[...] = rms_scale(before[...], gain[...]).astype(jnp.bfloat16)
        result = total
    else:
        normed, *group_refs, result, total = refs
    if far:
        half = group_refs[0].shape[0] // 2
        groups = [(r.at[pl.ds(0, half)], r.at[pl.ds(half, half)]) for r in group_refs]
    else:
        groups = list(zip(group_refs[::2], group_refs[1::2]))
    ahead = mxu(normed[...], groups[0][0][...], NT)
    for g in range(len(groups)):
        units = ahead
        if g + 1 < len(groups):
            ahead = mxu(normed[...], groups[g + 1][0][...], NT)
        added = mxu(jax.nn.gelu(units).astype(jnp.bfloat16), groups[g][1][...], NN)
        added = (before if g == 0 else total)[...] + added
        if g + 1 < len(groups):
            total[...] = added
        else:
            result[...] = added.astype(result.dtype)


def pairs_kernel(encoded, weights, pairs):
    pairs[...] = mxu(encoded[...], weights[...], NN).astype(jnp.bfloat16)


def decoder_kernel(first, own_pairs, other, weights, queries, out, other_pairs):
    rows = other.shape[0]
    part = rows // CH_DEV
    width = queries.shape[1]
    scale = float(HEAD_DIM) ** (-0.5)
    other_pairs[...] = mxu(other[...], weights[...], NN).astype(jnp.bfloat16)

    def span_pairs_of(span, col):
        return jnp.concatenate(
            [r[span * part : (span + 1) * part, col : col + HEAD_DIM] for r in (own_pairs, other_pairs)],
            axis=0,
        )

    for head in range(width // HEAD_DIM):
        col = head * HEAD_DIM
        query = (queries[:, col : col + HEAD_DIM].astype(jnp.float32) * scale).astype(jnp.bfloat16)
        scores = jnp.concatenate(
            [
                mxu(query[span * SPAN : (span + 1) * SPAN], span_pairs_of(span, col), NT)
                for span in range(CH_DEV)
            ],
            axis=0,
        )
        weights_f = jnp.exp(scores - jnp.max(scores, axis=1, keepdims=True))
        weights_f = weights_f / jnp.sum(weights_f, axis=1, keepdims=True)
        weights_b = weights_f.astype(jnp.bfloat16)
        for span in range(CH_DEV):
            result = mxu(
                weights_b[span * SPAN : (span + 1) * SPAN], span_pairs_of(span, width + col), NN
            )
            if span == 0:
                result = jnp.where(first[0] == 0, jnp.zeros_like(result), result)
            out[span * SPAN : (span + 1) * SPAN, col : col + HEAD_DIM] = result


def call(body, out_shape, in_specs, name, flops, vmem_mib, scratch=()):
    spaces = {"s": pltpu.SMEM, "v": pltpu.VMEM, "h": pl.ANY}
    return pl.pallas_call(
        body,
        out_shape=out_shape,
        in_specs=[pl.BlockSpec(memory_space=spaces[c]) for c in in_specs],
        out_specs=jax.tree.map(lambda _: pl.BlockSpec(memory_space=pltpu.VMEM), out_shape),
        scratch_shapes=list(scratch),
        compiler_params=pltpu.CompilerParams(vmem_limit_bytes=vmem_mib * 1024 * 1024),
        cost_estimate=pl.CostEstimate(flops=flops, bytes_accessed=8_000_000, transcendentals=0),
        name=name,
    )


def on_device(
    span_pairs,
    dec_queries,
    database,
    nbr_index,
    nbr_host,
    enc_gain,
    enc_query,
    enc_out,
    ffn_gain,
    ffn_up,
    ffn_down,
    dec_kv,
):
    seq_size = lax.axis_size("seq")
    lanes = lax.axis_size("mp")
    seq_index = lax.axis_index("seq")
    lane_index = lax.axis_index("mp")
    entries_here, block_rows, width = database.shape
    half_rows = block_rows // HALVES
    rows = CH_DEV * NEIGH * half_rows
    blocks = seq_size // 2
    far_lanes = lanes // 2 - 1

    def core_swap(array):
        return lax.ppermute(array, "mp", [(i, i ^ 1) for i in range(lanes)])

    def lane_step(array, step):
        return lax.ppermute(array, "mp", [(i, (i + 2 * step) % lanes) for i in range(lanes)])

    def seq_swap(array):
        return lax.ppermute(array, "seq", [(i, i ^ 1) for i in range(seq_size)])

    def seq_cross(array):
        return lax.ppermute(array, "seq", [(i, i ^ 2) for i in range(seq_size)])

    def seq_ring(array):
        return lax.ppermute(array, "seq", [(i, (i + 2) % seq_size) for i in range(seq_size)])

    def next_seq(array):
        return lax.ppermute(array, "seq", [(i, i + 1) for i in range(seq_size - 1)])

    def after(array, *others):
        return lax.optimization_barrier((array, *others))[0]

    query_t, up_t = enc_query.T, ffn_up.T
    kv_t = jnp.transpose(span_pairs, (1, 2, 0))
    kv_rows, tokens = kv_t.shape[1:]
    kept = tokens - SPAN

    here = seq_index.reshape(1).astype(jnp.int32)
    lane_here = lane_index.reshape(1).astype(jnp.int32)
    host, index = nbr_host.T, nbr_index.T
    dma = pltpu.SemaphoreType.DMA
    short = functools.partial(jax.ShapeDtypeStruct, dtype=jnp.bfloat16)
    database_half, attention_half, ffn_half, packet = call(
        prepare_kernel,
        (
            short((entries_here, half_rows, width)),
            short(enc_out.shape),
            short(ffn_down.shape),
            short((2, kv_rows + 16, SPAN)),
        ),
        "ssss" + "h" * 6,
        "prepare",
        rows * width,
        60,
        scratch=[
            pltpu.VMEM((entries_here, half_rows, width), jnp.float32),
            pltpu.VMEM((2, kv_rows, 2 * SPAN), jnp.bfloat16),
            dma((6,)),
        ],
    )(here, lane_here, host, index, database, query_t, enc_out, up_t, ffn_down, kv_t)

    attention_far = [lane_step(attention_half, n + 1) for n in range(far_lanes)]
    packet = next_seq(packet)
    database_ring = [database_half]
    for _ in range(blocks - 1):
        database_ring.append(seq_ring(database_ring[-1]))
    database_blocks = []
    for block in database_ring:
        database_blocks += [block, seq_swap(block)]

    dec_width = dec_kv.shape[2]
    kv_weights = dec_kv.reshape(width, 2 * dec_width)
    enc_gain, ffn_gain = enc_gain.reshape(1, width), ffn_gain.reshape(1, width)
    before = packet[:, kv_rows : kv_rows + 2, 0].astype(jnp.int32)
    before = before[:, :1] * DIGIT + before[:, 1:]
    kv_t = jnp.concatenate([packet[:, :kv_rows], kv_t[:, :, :kept]], axis=2)

    near_step = database_ring[min(1, blocks - 1)]
    ffn_far = [
        lane_step(after(ffn_half, near_step, database_blocks[1], *attention_far), n + 1)
        for n in range(far_lanes)
    ]
    attention_core = tuple(core_swap(a) for a in after((query_t, enc_out), database_ring[-1]))
    attention_cross = [seq_swap(after(a, *database_blocks)) for a in attention_far]
    kv_t, kv_weights, enc_gain, ffn_gain, before, *_ = lax.optimization_barrier(
        (kv_t, kv_weights, enc_gain, ffn_gain, before, database_blocks[min(3, 2 * blocks - 1)])
    )
    kv_core = core_swap(kv_t)
    kv_send = after(kv_t, *ffn_far, *database_blocks)
    kv_far = [lane_step(kv_send, n + 1) for n in range(far_lanes)]
    ffn_cross = [seq_cross(a) for a in ffn_far]
    up_send, down_send = after((up_t, ffn_down), *attention_cross)
    ffn_core = (core_swap(up_send), core_swap(down_send))

    gemm = 2 * rows * width * width
    long_rows = jax.ShapeDtypeStruct((rows, width), jnp.float32)
    short_rows = short((rows, width))
    values, normed = call(
        functools.partial(gather_kernel, blocks),
        (short_rows, short_rows),
        "ssss" + "v" * (1 + 2 * blocks),
        "neighbour_rows",
        10 * rows * width,
        16 + (8 * blocks * database_half.size >> 20),
    )(here, host, index, before, enc_gain, *database_blocks)

    def attention(so_far, weights, kv, far):
        return call(
            functools.partial(attention_kernel, len(kv), far),
            long_rows,
            "svv" + "v" * 3 * len(kv),
            "encoder_attention",
            gemm * 2 * len(kv) // lanes,
            24,
        )(here, so_far, normed, *weights, *kv)

    partial_rows = attention(values, (query_t, enc_out, *attention_core), (kv_t, kv_core), False)
    far_weights, far_kv = [], []
    kv_forward = after(tuple(kv_far), partial_rows)
    for straight, crossed, kv, forward in zip(attention_far, attention_cross, kv_far, kv_forward):
        far_weights += [straight, crossed, core_swap(straight), core_swap(crossed)]
        far_kv += [kv, core_swap(forward)]
    resid = attention(partial_rows, far_weights, far_kv, True)

    near_units = (up_t, ffn_down, *ffn_core)
    partial_rows, normed = call(
        functools.partial(ffn_kernel, False, True),
        (long_rows, short_rows),
        "vv" + "v" * len(near_units),
        "encoder_ffn_near",
        2 * gemm,
        30,
    )(ffn_gain, resid, *near_units)
    ffn_cross = after(tuple(ffn_cross), resid)
    far_units = [p for piece in [*ffn_far, *ffn_cross] for p in (piece, core_swap(piece))]
    encoded = call(
        functools.partial(ffn_kernel, True, False),
        short_rows,
        "vvv" + "v" * len(far_units),
        "encoder_ffn_far",
        2 * gemm,
        30,
        scratch=[pltpu.VMEM((rows, width), jnp.float32)],
    )(ffn_gain, partial_rows, normed, *far_units)

    other = core_swap(encoded)
    pairs_shape = (rows, 2 * dec_width)
    pairs_flops = 2 * rows * width * 2 * dec_width
    own_pairs = call(
        pairs_kernel,
        jax.ShapeDtypeStruct(pairs_shape, jnp.bfloat16),
        "vv",
        "decoder_pairs",
        pairs_flops,
        20,
    )(encoded, kv_weights)
    return call(
        decoder_kernel,
        jax.ShapeDtypeStruct(dec_queries.shape, jnp.float32),
        "svvvv",
        "decoder_attention",
        pairs_flops,
        28,
        scratch=[pltpu.VMEM(pairs_shape, jnp.bfloat16)],
    )(here, own_pairs, other, kv_weights, dec_queries)


def solution(mesh):
    placed = (
        P("seq", None, "mp"),
        P("seq", "mp"),
        P("seq", None, None),
        P("seq", None),
        P("seq", None),
        P(),
        P(None, "mp"),
        P("mp", None),
        P(),
        P(None, "mp"),
        P("mp", None),
        P(None, None, "mp"),
    )
    return jax.shard_map(
        on_device, mesh=mesh, in_specs=placed, out_specs=P("seq", "mp"), check_vma=False
    )
```

```python
import functools

import jax
import jax.numpy as jnp
from jax import lax
from jax.experimental import pallas as pl
from jax.experimental.pallas import tpu as pltpu
from jax.sharding import PartitionSpec as P

HEAD_DIM = 128
EHEAD_DIM = 112
SPAN = 64
NBL = 128
NEIGH = 2
CH_DEV = 8
HALVES = 2
BLOCK = 512
DIGIT = 128

NT = (((1,), (1,)), ((), ()))
NN = (((1,), (0,)), ((), ()))


def mxu(lhs, rhs, dims):
    return lax.dot_general(lhs, rhs, dims, preferred_element_type=jnp.float32)


def rms_scale(values, gain):
    return values * lax.rsqrt(jnp.mean(values * values, axis=-1, keepdims=True) + 1e-06) * gain


def turned(chunk):
    return jnp.concatenate([chunk[:, SPAN:], chunk[:, :SPAN]], axis=1)


def prepare_kernel(here, lane_here, host, index, database, query_t, enc_out, up_t, down, kv_t, *refs):
    db_half, attention_half, ffn_half, packet, db_in, kv_in, sems = refs
    per_host, half_rows, width = db_half.shape
    seq, lane = here[0], lane_here[0]
    copies = [
        pltpu.make_async_copy(
            database.at[:, pl.ds(pl.multiple_of(lane % HALVES * half_rows, half_rows), half_rows)],
            db_in,
            sems.at[0],
        ),
        pltpu.make_async_copy(kv_t.at[:, :, pl.ds(kv_t.shape[2] - 2 * SPAN, 2 * SPAN)], kv_in, sems.at[1]),
    ]
    halves = ((query_t, attention_half, 0, seq % 2), (enc_out, attention_half, 1, seq % 2))
    halves += ((up_t, ffn_half, 0, seq // 2 % 2), (down, ffn_half, 1, seq // 2 % 2))
    for i, (source, target, spot, parity) in enumerate(halves):
        count = source.shape[0] // 2
        copies.append(
            pltpu.make_async_copy(
                source.at[pl.ds(pl.multiple_of(parity * count, 16), count)],
                target.at[pl.ds(spot * count, count)],
                sems.at[2 + i],
            )
        )
    for copy in copies:
        copy.start()
    copies[0].wait()
    db_half[...] = db_in[...].astype(jnp.bfloat16)
    copies[1].wait()
    kv_rows = kv_in.shape[1]
    row = lax.broadcasted_iota(jnp.int32, (packet.shape[1] - kv_rows, SPAN), 0)
    for k in range(NEIGH):
        entry = host[k, CH_DEV - 1] * per_host + index[k, CH_DEV - 1]
        digits = jnp.where(row == 0, entry // DIGIT, jnp.where(row == 1, entry % DIGIT, 0))
        packet[k, :kv_rows, :] = kv_in[k][:, SPAN:]
        packet[k, kv_rows:, :] = digits.astype(jnp.float32).astype(jnp.bfloat16)
    for copy in copies[2:]:
        copy.wait()


def gather_kernel(blocks, here, host, index, before, gain, *refs):
    *db_refs, rows_out, normed_out = refs
    per_host, part_rows, width = db_refs[0].shape
    seq = here[0]
    for i in range(CH_DEV * NEIGH):
        span, k = i // NEIGH, i % NEIGH
        if span == 0:
            of_host, place = before[k, 0] // per_host, before[k, 0] % per_host
        else:
            of_host, place = host[k, span - 1], index[k, span - 1]
        block = (seq // 2 - of_host // 2 + blocks) % blocks * 2 + (seq + of_host) % 2
        for b in range(2 * blocks):

            @pl.when(block == b)
            def _(b=b, place=place, i=i):
                rows_out[i * part_rows : (i + 1) * part_rows, :] = db_refs[b][place]

    values = rows_out[...].astype(jnp.float32)
    normed_out[...] = rms_scale(values, gain[...]).astype(jnp.bfloat16)


def attention_kernel(pieces, far, seq_index, before, normed_in, *refs):
    weight_refs, kv_refs, (result,) = refs[: 2 * pieces], refs[2 * pieces : 3 * pieces], refs[3 * pieces :]
    rows, width = before.shape
    span_rows = rows // CH_DEV
    pair_rows = 2 * span_rows
    pad = HEAD_DIM - EHEAD_DIM
    scale = float(EHEAD_DIM) ** (-0.5)
    odd = seq_index[0] % 2
    lane = lax.broadcasted_iota(jnp.int32, (pair_rows, 2 * SPAN), 1)
    row = lax.broadcasted_iota(jnp.int32, (pair_rows, 2 * SPAN), 0)
    own_lanes = (lane < SPAN) == (row < span_rows)
    rest = jnp.zeros((pad, 2 * SPAN), jnp.bfloat16)
    empty = jnp.zeros((HEAD_DIM, 2 * SPAN), jnp.bfloat16)
    ones = jnp.ones((2 * HEAD_DIM - EHEAD_DIM, 2 * SPAN), jnp.bfloat16)
    weight_rest = jnp.zeros((pad, width), jnp.bfloat16)
    for p in range(pieces):
        first, second = weight_refs[2 * p][...], weight_refs[2 * p + 1][...]
        if far:
            first, second = (
                jnp.where(odd == 0, first, second),
                jnp.where(odd == 0, second, first),
            )
            q_parts = (first[:EHEAD_DIM], second[:EHEAD_DIM])
            out_parts = (first[EHEAD_DIM:], second[EHEAD_DIM:])
        else:
            q_parts = (first[:EHEAD_DIM], first[EHEAD_DIM:])
            out_parts = (second[:EHEAD_DIM], second[EHEAD_DIM:])
        q_w = jnp.concatenate([q_parts[0], weight_rest, q_parts[1], weight_rest], axis=0)
        out_w = jnp.concatenate([out_parts[0], weight_rest, out_parts[1], weight_rest], axis=0)
        for start in range(0, rows, BLOCK):
            block = slice(start, start + BLOCK)
            query = (mxu(normed_in[block, :], q_w, NT) * scale).astype(jnp.bfloat16)
            scores = []
            for at in range(0, BLOCK, pair_rows):
                tok = (start + at) // pair_rows * 2 * SPAN
                keys = kv_refs[p][0, :, tok : tok + 2 * SPAN]
                keys = jnp.concatenate(
                    [
                        jnp.concatenate([keys[:EHEAD_DIM], rest, empty], axis=0),
                        jnp.concatenate([empty, turned(keys[EHEAD_DIM:]), rest], axis=0),
                    ],
                    axis=1,
                )
                both = mxu(query[at : at + pair_rows], keys, NN)
                scores.append(jnp.where(own_lanes, both[:, : 2 * SPAN], both[:, 2 * SPAN :]))
            scores = jnp.concatenate(scores, axis=0)
            left = lax.broadcasted_iota(jnp.int32, scores.shape, 1) < SPAN
            low = jnp.max(jnp.where(left, scores, -jnp.inf), axis=1, keepdims=True)
            high = jnp.max(jnp.where(left, -jnp.inf, scores), axis=1, keepdims=True)
            weights = jnp.exp(scores - jnp.where(left, low, high)).astype(jnp.bfloat16)
            attended = []
            for at in range(0, BLOCK, pair_rows):
                tok = (start + at) // pair_rows * 2 * SPAN
                part = weights[at : at + pair_rows]
                vals = kv_refs[p][1, :, tok : tok + 2 * SPAN]
                heads = []
                for head in range(2):
                    picked = jnp.where(own_lanes if head == 0 else ~own_lanes, part, jnp.zeros_like(part))
                    of_head = vals[:EHEAD_DIM] if head == 0 else turned(vals[EHEAD_DIM:])
                    mixed = mxu(picked, jnp.concatenate([of_head, ones], axis=0), NT)
                    heads.append((mixed[:, :HEAD_DIM] / mixed[:, HEAD_DIM:]).astype(jnp.bfloat16))
                attended.append(jnp.concatenate(heads, axis=1))
            so_far = before if p == 0 else result
            result[block, :] = so_far[block, :].astype(jnp.float32) + mxu(jnp.concatenate(attended, axis=0), out_w, NN)


def ffn_kernel(far, first, gain, before, *refs):
    if first:
        *group_refs, total, normed = refs
        normed[...] = rms_scale(before[...], gain[...]).astype(jnp.bfloat16)
        result = total
    else:
        normed, *group_refs, result, total = refs
    if far:
        half = group_refs[0].shape[0] // 2
        groups = [(r.at[pl.ds(0, half)], r.at[pl.ds(half, half)]) for r in group_refs]
    else:
        groups = list(zip(group_refs[::2], group_refs[1::2]))
    ahead = mxu(normed[...], groups[0][0][...], NT)
    for g in range(len(groups)):
        units = ahead
        if g + 1 < len(groups):
            ahead = mxu(normed[...], groups[g + 1][0][...], NT)
        added = mxu(jax.nn.gelu(units).astype(jnp.bfloat16), groups[g][1][...], NN)
        added = (before if g == 0 else total)[...] + added
        if g + 1 < len(groups):
            total[...] = added
        else:
            result[...] = added.astype(result.dtype)


def pairs_kernel(encoded, weights, pairs):
    pairs[...] = mxu(encoded[...], weights[...], NN).astype(jnp.bfloat16)


def decoder_kernel(first, own_pairs, other, weights, queries, out, other_pairs):
    rows = other.shape[0]
    part = rows // CH_DEV
    width = queries.shape[1]
    scale = float(HEAD_DIM) ** (-0.5)
    other_pairs[...] = mxu(other[...], weights[...], NN).astype(jnp.bfloat16)

    def span_pairs_of(span, col):
        return jnp.concatenate(
            [r[span * part : (span + 1) * part, col : col + HEAD_DIM] for r in (own_pairs, other_pairs)],
            axis=0,
        )

    ones = jnp.ones((2 * part, HEAD_DIM), jnp.bfloat16)
    for head in range(width // HEAD_DIM):
        col = head * HEAD_DIM
        query = (queries[:, col : col + HEAD_DIM].astype(jnp.float32) * scale).astype(jnp.bfloat16)
        scores = jnp.concatenate(
            [
                mxu(query[span * SPAN : (span + 1) * SPAN], span_pairs_of(span, col), NT)
                for span in range(CH_DEV)
            ],
            axis=0,
        )
        weights_b = jnp.exp(scores - jnp.max(scores, axis=1, keepdims=True)).astype(jnp.bfloat16)
        for span in range(CH_DEV):
            vals = jnp.concatenate([span_pairs_of(span, width + col), ones], axis=1)
            result = mxu(weights_b[span * SPAN : (span + 1) * SPAN], vals, NN)
            result = result[:, :HEAD_DIM] / result[:, HEAD_DIM:]
            if span == 0:
                result = jnp.where(first[0] == 0, jnp.zeros_like(result), result)
            out[span * SPAN : (span + 1) * SPAN, col : col + HEAD_DIM] = result


def call(body, out_shape, in_specs, name, flops, vmem_mib, scratch=()):
    spaces = {"s": pltpu.SMEM, "v": pltpu.VMEM, "h": pl.ANY}
    return pl.pallas_call(
        body,
        out_shape=out_shape,
        in_specs=[pl.BlockSpec(memory_space=spaces[c]) for c in in_specs],
        out_specs=jax.tree.map(lambda _: pl.BlockSpec(memory_space=pltpu.VMEM), out_shape),
        scratch_shapes=list(scratch),
        compiler_params=pltpu.CompilerParams(vmem_limit_bytes=vmem_mib * 1024 * 1024),
        cost_estimate=pl.CostEstimate(flops=flops, bytes_accessed=8_000_000, transcendentals=0),
        name=name,
    )


def on_device(
    span_pairs,
    dec_queries,
    database,
    nbr_index,
    nbr_host,
    enc_gain,
    enc_query,
    enc_out,
    ffn_gain,
    ffn_up,
    ffn_down,
    dec_kv,
):
    seq_size = lax.axis_size("seq")
    lanes = lax.axis_size("mp")
    seq_index = lax.axis_index("seq")
    lane_index = lax.axis_index("mp")
    entries_here, block_rows, width = database.shape
    half_rows = block_rows // HALVES
    rows = CH_DEV * NEIGH * half_rows
    blocks = seq_size // 2
    far_lanes = lanes // 2 - 1

    def core_swap(array):
        return lax.ppermute(array, "mp", [(i, i ^ 1) for i in range(lanes)])

    def lane_step(array, step):
        return lax.ppermute(array, "mp", [(i, (i + 2 * step) % lanes) for i in range(lanes)])

    def seq_swap(array):
        return lax.ppermute(array, "seq", [(i, i ^ 1) for i in range(seq_size)])

    def seq_cross(array):
        return lax.ppermute(array, "seq", [(i, i ^ 2) for i in range(seq_size)])

    def seq_ring(array, way):
        return lax.ppermute(array, "seq", [(i, (i + 2 * way) % seq_size) for i in range(seq_size)])

    def next_seq(array):
        return lax.ppermute(array, "seq", [(i, i + 1) for i in range(seq_size - 1)])

    def after(array, *others):
        return lax.optimization_barrier((array, *others))[0]

    query_t, up_t = enc_query.T, ffn_up.T
    kv_t = jnp.transpose(span_pairs, (1, 2, 0))
    kv_rows, tokens = kv_t.shape[1:]
    kept = tokens - SPAN

    here = seq_index.reshape(1).astype(jnp.int32)
    lane_here = lane_index.reshape(1).astype(jnp.int32)
    host, index = nbr_host.T, nbr_index.T
    dma = pltpu.SemaphoreType.DMA
    short = functools.partial(jax.ShapeDtypeStruct, dtype=jnp.bfloat16)
    database_half, attention_half, ffn_half, packet = call(
        prepare_kernel,
        (
            short((entries_here, half_rows, width)),
            short(enc_out.shape),
            short(ffn_down.shape),
            short((2, kv_rows + 16, SPAN)),
        ),
        "ssss" + "h" * 6,
        "prepare",
        rows * width,
        60,
        scratch=[
            pltpu.VMEM((entries_here, half_rows, width), jnp.float32),
            pltpu.VMEM((2, kv_rows, 2 * SPAN), jnp.bfloat16),
            dma((6,)),
        ],
    )(here, lane_here, host, index, database, query_t, enc_out, up_t, ffn_down, kv_t)

    attention_far = [lane_step(attention_half, n + 1) for n in range(far_lanes)]
    database_far = [database_half] + [None] * (blocks - 1)
    for step in range(1, blocks // 2 + 1):
        database_far[step] = seq_ring(database_far[step - 1], 1)
        if blocks - step > blocks // 2:
            database_far[blocks - step] = seq_ring(database_far[(blocks - step + 1) % blocks], -1)
    database_blocks = []
    for block in database_far:
        database_blocks += [block, seq_swap(block)]
    packet = next_seq(after(packet, database_blocks[1], database_far[1]))
    ffn_half = after(ffn_half, *attention_far)
    ffn_far = [lane_step(ffn_half, n + 1) for n in range(far_lanes)]

    dec_width = dec_kv.shape[2]
    kv_weights = dec_kv.reshape(width, 2 * dec_width)
    enc_gain, ffn_gain = enc_gain.reshape(1, width), ffn_gain.reshape(1, width)
    before = packet[:, kv_rows : kv_rows + 2, 0].astype(jnp.int32)
    before = before[:, :1] * DIGIT + before[:, 1:]
    kv_t = jnp.concatenate([packet[:, :kv_rows], kv_t[:, :, :kept]], axis=2)

    attention_core = tuple(core_swap(a) for a in after((query_t, enc_out), database_blocks[3]))
    attention_cross = [seq_swap(after(a, database_blocks[-1])) for a in attention_far]
    kv_t, kv_weights, enc_gain, ffn_gain, before, *_ = lax.optimization_barrier(
        (kv_t, kv_weights, enc_gain, ffn_gain, before, database_blocks[3], database_blocks[-1])
    )
    kv_core = core_swap(kv_t)
    kv_send = after(kv_t, *ffn_far)
    kv_far = [lane_step(kv_send, n + 1) for n in range(far_lanes)]
    ffn_cross = [seq_cross(a) for a in ffn_far]
    up_send, down_send = after((up_t, ffn_down), database_blocks[3])
    ffn_core = (core_swap(up_send), core_swap(down_send))

    gemm = 2 * rows * width * width
    long_rows = jax.ShapeDtypeStruct((rows, width), jnp.float32)
    short_rows = short((rows, width))
    values, normed = call(
        functools.partial(gather_kernel, blocks),
        (short_rows, short_rows),
        "ssss" + "v" * (1 + 2 * blocks),
        "neighbour_rows",
        10 * rows * width,
        16 + (8 * blocks * database_half.size >> 20),
    )(here, host, index, before, enc_gain, *database_blocks)

    def attention(so_far, weights, kv, far):
        return call(
            functools.partial(attention_kernel, len(kv), far),
            long_rows,
            "svv" + "v" * 3 * len(kv),
            "encoder_attention",
            gemm * 2 * len(kv) // lanes,
            24,
        )(here, so_far, normed, *weights, *kv)

    partial_rows = attention(values, (query_t, enc_out, *attention_core), (kv_t, kv_core), False)
    far_weights, far_kv = [], []
    kv_forward = after(tuple(kv_far), partial_rows)
    for straight, crossed, kv, forward in zip(attention_far, attention_cross, kv_far, kv_forward):
        far_weights += [straight, crossed, core_swap(straight), core_swap(crossed)]
        far_kv += [kv, core_swap(forward)]
    resid = attention(partial_rows, far_weights, far_kv, True)

    near_units = (up_t, ffn_down, *ffn_core)
    partial_rows, normed = call(
        functools.partial(ffn_kernel, False, True),
        (long_rows, short_rows),
        "vv" + "v" * len(near_units),
        "encoder_ffn_near",
        2 * gemm,
        30,
    )(ffn_gain, resid, *near_units)
    ffn_cross = after(tuple(ffn_cross), resid)
    far_units = [p for piece in [*ffn_far, *ffn_cross] for p in (piece, core_swap(piece))]
    encoded = call(
        functools.partial(ffn_kernel, True, False),
        short_rows,
        "vvv" + "v" * len(far_units),
        "encoder_ffn_far",
        2 * gemm,
        30,
        scratch=[pltpu.VMEM((rows, width), jnp.float32)],
    )(ffn_gain, partial_rows, normed, *far_units)

    other = core_swap(encoded)
    pairs_shape = (rows, 2 * dec_width)
    pairs_flops = 2 * rows * width * 2 * dec_width
    own_pairs = call(
        pairs_kernel,
        jax.ShapeDtypeStruct(pairs_shape, jnp.bfloat16),
        "vv",
        "decoder_pairs",
        pairs_flops,
        20,
    )(encoded, kv_weights)
    return call(
        decoder_kernel,
        jax.ShapeDtypeStruct(dec_queries.shape, jnp.float32),
        "svvvv",
        "decoder_attention",
        pairs_flops,
        28,
        scratch=[pltpu.VMEM(pairs_shape, jnp.bfloat16)],
    )(here, own_pairs, other, kv_weights, dec_queries)


def solution(mesh):
    placed = (
        P("seq", None, "mp"),
        P("seq", "mp"),
        P("seq", None, None),
        P("seq", None),
        P("seq", None),
        P(),
        P(None, "mp"),
        P("mp", None),
        P(),
        P(None, "mp"),
        P("mp", None),
        P(None, None, "mp"),
    )
    return jax.shard_map(
        on_device, mesh=mesh, in_specs=placed, out_specs=P("seq", "mp"), check_vma=False
    )
```

```python
import functools

import jax
import jax.numpy as jnp
from jax import lax
from jax.experimental import pallas as pl
from jax.experimental.pallas import tpu as pltpu
from jax.sharding import PartitionSpec as P

HEAD_DIM = 128
EHEAD_DIM = 112
SPAN = 64
NBL = 128
NEIGH = 2
CH_DEV = 8
HALVES = 2
BLOCK = 512
DIGIT = 128

ORDER = {
    "pk": ("x0",),
    "xp": ("xn",),
    "xa": ("xm",),
    "ca": ("xn",),
    "cf": ("xn",),
    "keys": ("xp",),
    "yk": ("yf", "xm",),
    "cya": ("yf",),
    "cyf": ("far",),
    "cyk": ("near",),
    "czf": ("far",),
    "near": ("yf",),
    "wk": ("ya",),
    "gains": ("zn",),
}

NT = (((1,), (1,)), ((), ()))
NN = (((1,), (0,)), ((), ()))


def mxu(lhs, rhs, dims):
    return lax.dot_general(lhs, rhs, dims, preferred_element_type=jnp.float32)


def rms_scale(values, gain):
    return values * lax.rsqrt(jnp.mean(values * values, axis=-1, keepdims=True) + 1e-06) * gain


def turned(chunk):
    return jnp.concatenate([chunk[:, SPAN:], chunk[:, :SPAN]], axis=1)


def prepare_kernel(here, lane_here, host, index, database, query_t, enc_out, up_t, down, kv_t, *refs):
    db_half, attention_half, ffn_half, packet, db_in, kv_in, sems = refs
    per_host, half_rows, width = db_half.shape
    seq, lane = here[0], lane_here[0]
    copies = [
        pltpu.make_async_copy(
            database.at[:, pl.ds(pl.multiple_of(lane % HALVES * half_rows, half_rows), half_rows)],
            db_in,
            sems.at[0],
        ),
        pltpu.make_async_copy(kv_t.at[:, :, pl.ds(kv_t.shape[2] - 2 * SPAN, 2 * SPAN)], kv_in, sems.at[1]),
    ]
    halves = ((query_t, attention_half, 0, seq % 2), (enc_out, attention_half, 1, seq % 2))
    halves += ((up_t, ffn_half, 0, seq // 2 % 2), (down, ffn_half, 1, seq // 2 % 2))
    for i, (source, target, spot, parity) in enumerate(halves):
        count = source.shape[0] // 2
        copies.append(
            pltpu.make_async_copy(
                source.at[pl.ds(pl.multiple_of(parity * count, 16), count)],
                target.at[pl.ds(spot * count, count)],
                sems.at[2 + i],
            )
        )
    for copy in copies:
        copy.start()
    copies[0].wait()
    db_half[...] = db_in[...].astype(jnp.bfloat16)
    copies[1].wait()
    kv_rows = kv_in.shape[1]
    row = lax.broadcasted_iota(jnp.int32, (packet.shape[1] - kv_rows, SPAN), 0)
    for k in range(NEIGH):
        entry = host[k, CH_DEV - 1] * per_host + index[k, CH_DEV - 1]
        digits = jnp.where(row == 0, entry // DIGIT, jnp.where(row == 1, entry % DIGIT, 0))
        packet[k, :kv_rows, :] = kv_in[k][:, SPAN:]
        packet[k, kv_rows:, :] = digits.astype(jnp.float32).astype(jnp.bfloat16)
    for copy in copies[2:]:
        copy.wait()


def gather_kernel(blocks, here, host, index, before, gain, *refs):
    *db_refs, rows_out, normed_out = refs
    per_host, part_rows, width = db_refs[0].shape
    seq = here[0]
    for i in range(CH_DEV * NEIGH):
        span, k = i // NEIGH, i % NEIGH
        if span == 0:
            of_host, place = before[k, 0] // per_host, before[k, 0] % per_host
        else:
            of_host, place = host[k, span - 1], index[k, span - 1]
        block = (seq // 2 - of_host // 2 + blocks) % blocks * 2 + (seq + of_host) % 2
        for b in range(2 * blocks):

            @pl.when(block == b)
            def _(b=b, place=place, i=i):
                rows_out[i * part_rows : (i + 1) * part_rows, :] = db_refs[b][place]

    values = rows_out[...].astype(jnp.float32)
    normed_out[...] = rms_scale(values, gain[...]).astype(jnp.bfloat16)


def attention_kernel(pieces, far, seq_index, before, normed_in, *refs):
    weight_refs, kv_refs, (result,) = refs[: 2 * pieces], refs[2 * pieces : 3 * pieces], refs[3 * pieces :]
    rows, width = before.shape
    span_rows = rows // CH_DEV
    pair_rows = 2 * span_rows
    pad = HEAD_DIM - EHEAD_DIM
    scale = float(EHEAD_DIM) ** (-0.5)
    odd = seq_index[0] % 2
    lane = lax.broadcasted_iota(jnp.int32, (pair_rows, 2 * SPAN), 1)
    row = lax.broadcasted_iota(jnp.int32, (pair_rows, 2 * SPAN), 0)
    own_lanes = (lane < SPAN) == (row < span_rows)
    rest = jnp.zeros((pad, 2 * SPAN), jnp.bfloat16)
    empty = jnp.zeros((HEAD_DIM, 2 * SPAN), jnp.bfloat16)
    ones = jnp.ones((2 * HEAD_DIM - EHEAD_DIM, 2 * SPAN), jnp.bfloat16)
    weight_rest = jnp.zeros((pad, width), jnp.bfloat16)
    for p in range(pieces):
        first, second = weight_refs[2 * p][...], weight_refs[2 * p + 1][...]
        if far:
            first, second = (
                jnp.where(odd == 0, first, second),
                jnp.where(odd == 0, second, first),
            )
            q_parts = (first[:EHEAD_DIM], second[:EHEAD_DIM])
            out_parts = (first[EHEAD_DIM:], second[EHEAD_DIM:])
        else:
            q_parts = (first[:EHEAD_DIM], first[EHEAD_DIM:])
            out_parts = (second[:EHEAD_DIM], second[EHEAD_DIM:])
        q_w = jnp.concatenate([q_parts[0], weight_rest, q_parts[1], weight_rest], axis=0)
        out_w = jnp.concatenate([out_parts[0], weight_rest, out_parts[1], weight_rest], axis=0)
        for start in range(0, rows, BLOCK):
            block = slice(start, start + BLOCK)
            query = (mxu(normed_in[block, :], q_w, NT) * scale).astype(jnp.bfloat16)
            scores = []
            for at in range(0, BLOCK, pair_rows):
                tok = (start + at) // pair_rows * 2 * SPAN
                keys = kv_refs[p][0, :, tok : tok + 2 * SPAN]
                keys = jnp.concatenate(
                    [
                        jnp.concatenate([keys[:EHEAD_DIM], rest, empty], axis=0),
                        jnp.concatenate([empty, turned(keys[EHEAD_DIM:]), rest], axis=0),
                    ],
                    axis=1,
                )
                both = mxu(query[at : at + pair_rows], keys, NN)
                scores.append(jnp.where(own_lanes, both[:, : 2 * SPAN], both[:, 2 * SPAN :]))
            scores = jnp.concatenate(scores, axis=0)
            left = lax.broadcasted_iota(jnp.int32, scores.shape, 1) < SPAN
            low = jnp.max(jnp.where(left, scores, -jnp.inf), axis=1, keepdims=True)
            high = jnp.max(jnp.where(left, -jnp.inf, scores), axis=1, keepdims=True)
            weights = jnp.exp(scores - jnp.where(left, low, high)).astype(jnp.bfloat16)
            attended = []
            for at in range(0, BLOCK, pair_rows):
                tok = (start + at) // pair_rows * 2 * SPAN
                part = weights[at : at + pair_rows]
                vals = kv_refs[p][1, :, tok : tok + 2 * SPAN]
                heads = []
                for head in range(2):
                    picked = jnp.where(own_lanes if head == 0 else ~own_lanes, part, jnp.zeros_like(part))
                    of_head = vals[:EHEAD_DIM] if head == 0 else turned(vals[EHEAD_DIM:])
                    mixed = mxu(picked, jnp.concatenate([of_head, ones], axis=0), NT)
                    heads.append((mixed[:, :HEAD_DIM] / mixed[:, HEAD_DIM:]).astype(jnp.bfloat16))
                attended.append(jnp.concatenate(heads, axis=1))
            so_far = before if p == 0 else result
            result[block, :] = so_far[block, :].astype(jnp.float32) + mxu(jnp.concatenate(attended, axis=0), out_w, NN)


def ffn_kernel(far, first, gain, before, *refs):
    if first:
        *group_refs, total, normed = refs
        normed[...] = rms_scale(before[...], gain[...]).astype(jnp.bfloat16)
        result = total
    else:
        normed, *group_refs, result, total = refs
    if far:
        half = group_refs[0].shape[0] // 2
        groups = [(r.at[pl.ds(0, half)], r.at[pl.ds(half, half)]) for r in group_refs]
    else:
        groups = list(zip(group_refs[::2], group_refs[1::2]))
    ahead = mxu(normed[...], groups[0][0][...], NT)
    for g in range(len(groups)):
        units = ahead
        if g + 1 < len(groups):
            ahead = mxu(normed[...], groups[g + 1][0][...], NT)
        added = mxu(jax.nn.gelu(units).astype(jnp.bfloat16), groups[g][1][...], NN)
        added = (before if g == 0 else total)[...] + added
        if g + 1 < len(groups):
            total[...] = added
        else:
            result[...] = added.astype(result.dtype)


def pairs_kernel(encoded, weights, pairs):
    pairs[...] = mxu(encoded[...], weights[...], NN).astype(jnp.bfloat16)


def decoder_kernel(first, own_pairs, other, weights, queries, out, other_pairs):
    rows = other.shape[0]
    part = rows // CH_DEV
    width = queries.shape[1]
    scale = float(HEAD_DIM) ** (-0.5)
    other_pairs[...] = mxu(other[...], weights[...], NN).astype(jnp.bfloat16)

    def span_pairs_of(span, col):
        return jnp.concatenate(
            [r[span * part : (span + 1) * part, col : col + HEAD_DIM] for r in (own_pairs, other_pairs)],
            axis=0,
        )

    ones = jnp.ones((2 * part, HEAD_DIM), jnp.bfloat16)
    for head in range(width // HEAD_DIM):
        col = head * HEAD_DIM
        query = (queries[:, col : col + HEAD_DIM].astype(jnp.float32) * scale).astype(jnp.bfloat16)
        scores = jnp.concatenate(
            [
                mxu(query[span * SPAN : (span + 1) * SPAN], span_pairs_of(span, col), NT)
                for span in range(CH_DEV)
            ],
            axis=0,
        )
        weights_b = jnp.exp(scores - jnp.max(scores, axis=1, keepdims=True)).astype(jnp.bfloat16)
        for span in range(CH_DEV):
            vals = jnp.concatenate([span_pairs_of(span, width + col), ones], axis=1)
            result = mxu(weights_b[span * SPAN : (span + 1) * SPAN], vals, NN)
            result = result[:, :HEAD_DIM] / result[:, HEAD_DIM:]
            if span == 0:
                result = jnp.where(first[0] == 0, jnp.zeros_like(result), result)
            out[span * SPAN : (span + 1) * SPAN, col : col + HEAD_DIM] = result


def call(body, out_shape, in_specs, name, flops, vmem_mib, scratch=()):
    spaces = {"s": pltpu.SMEM, "v": pltpu.VMEM, "h": pl.ANY}
    return pl.pallas_call(
        body,
        out_shape=out_shape,
        in_specs=[pl.BlockSpec(memory_space=spaces[c]) for c in in_specs],
        out_specs=jax.tree.map(lambda _: pl.BlockSpec(memory_space=pltpu.VMEM), out_shape),
        scratch_shapes=list(scratch),
        compiler_params=pltpu.CompilerParams(vmem_limit_bytes=vmem_mib * 1024 * 1024),
        cost_estimate=pl.CostEstimate(flops=flops, bytes_accessed=8_000_000, transcendentals=0),
        name=name,
    )


def on_device(
    span_pairs,
    dec_queries,
    database,
    nbr_index,
    nbr_host,
    enc_gain,
    enc_query,
    enc_out,
    ffn_gain,
    ffn_up,
    ffn_down,
    dec_kv,
):
    seq_size = lax.axis_size("seq")
    lanes = lax.axis_size("mp")
    seq_index = lax.axis_index("seq")
    lane_index = lax.axis_index("mp")
    entries_here, block_rows, width = database.shape
    half_rows = block_rows // HALVES
    rows = CH_DEV * NEIGH * half_rows
    blocks = seq_size // 2

    def core_swap(array):
        return lax.ppermute(array, "mp", [(i, i ^ 1) for i in range(lanes)])

    def lane_step(array, step):
        return lax.ppermute(array, "mp", [(i, (i + 2 * step) % lanes) for i in range(lanes)])

    def seq_swap(array):
        return lax.ppermute(array, "seq", [(i, i ^ 1) for i in range(seq_size)])

    def seq_cross(array):
        return lax.ppermute(array, "seq", [(i, i ^ 2) for i in range(seq_size)])

    def seq_ring(array, way):
        return lax.ppermute(array, "seq", [(i, (i + 2 * way) % seq_size) for i in range(seq_size)])

    def next_seq(array):
        return lax.ppermute(array, "seq", [(i, i + 1) for i in range(seq_size - 1)])

    query_t, up_t = enc_query.T, ffn_up.T
    kv_t = jnp.transpose(span_pairs, (1, 2, 0))
    kv_rows, tokens = kv_t.shape[1:]
    kept = tokens - SPAN

    here = seq_index.reshape(1).astype(jnp.int32)
    lane_here = lane_index.reshape(1).astype(jnp.int32)
    host, index = nbr_host.T, nbr_index.T
    dma = pltpu.SemaphoreType.DMA
    short = functools.partial(jax.ShapeDtypeStruct, dtype=jnp.bfloat16)
    database_half, attention_half, ffn_half, packet = call(
        prepare_kernel,
        (
            short((entries_here, half_rows, width)),
            short(enc_out.shape),
            short(ffn_down.shape),
            short((2, kv_rows + 16, SPAN)),
        ),
        "ssss" + "h" * 6,
        "prepare",
        rows * width,
        60,
        scratch=[
            pltpu.VMEM((entries_here, half_rows, width), jnp.float32),
            pltpu.VMEM((2, kv_rows, 2 * SPAN), jnp.bfloat16),
            dma((6,)),
        ],
    )(here, lane_here, host, index, database, query_t, enc_out, up_t, ffn_down, kv_t)

    dec_width = dec_kv.shape[2]
    middle, last = blocks // 2, blocks - 1
    names = {"0": 0, "n": 1, "p": last, "m": middle}
    short_name = {place: name for name, place in names.items()}
    arrived = {}

    def got(name):
        if name not in arrived:
            arrived[name] = makers[name]()
        return arrived[name]

    def ready(name, array):
        others = [got(other) for other in ORDER.get(name, ())]
        return lax.optimization_barrier((array, others))[0] if others else array

    def database(place):
        if place == 0:
            return database_half
        way = 1 if place <= middle else -1
        source = database_at((place - way) % blocks)
        return seq_ring(ready(f"z{short_name.get(place, place)}", source), way)

    def database_at(place):
        return got(f"z{short_name.get(place, place)}")

    def swapped_at(place):
        return got(f"x{short_name.get(place, place)}")

    def received_keys():
        return jnp.concatenate([got("pk")[:, :kv_rows], kv_t[:, :, :kept]], axis=2)

    def both_cores(name, arrays):
        return tuple(core_swap(a) for a in ready(name, arrays))

    makers = {
        "ya": lambda: lane_step(ready("ya", attention_half), 1),
        "yf": lambda: lane_step(ready("yf", ffn_half), 1),
        "yk": lambda: lane_step(ready("yk", got("keys")), 1),
        "pk": lambda: next_seq(ready("pk", packet)),
        "keys": lambda: ready("keys", received_keys()),
        "xa": lambda: seq_swap(ready("xa", got("ya"))),
        "zf": lambda: seq_cross(ready("zf", got("yf"))),
        "ca": lambda: both_cores("ca", (query_t, enc_out)),
        "cf": lambda: both_cores("cf", (up_t, ffn_down)),
        "ck": lambda: core_swap(ready("ck", got("keys"))),
        "cya": lambda: core_swap(ready("cya", got("ya"))),
        "cyk": lambda: core_swap(ready("cyk", got("yk"))),
        "cyf": lambda: core_swap(ready("cyf", got("yf"))),
        "cxa": lambda: core_swap(ready("cxa", got("xa"))),
        "czf": lambda: core_swap(ready("czf", got("zf"))),
        "wk": lambda: ready("wk", dec_kv.reshape(width, 2 * dec_width)),
    }
    for place in range(blocks):
        name = short_name.get(place, place)
        makers[f"z{name}"] = functools.partial(database, place)
        makers[f"x{name}"] = lambda place=place, name=name: seq_swap(ready(f"x{name}", database_at(place)))
    enc_gain, ffn_gain = enc_gain.reshape(1, width), ffn_gain.reshape(1, width)
    enc_gain, ffn_gain = ready("gains", (enc_gain, ffn_gain))

    gemm = 2 * rows * width * width
    long_rows = jax.ShapeDtypeStruct((rows, width), jnp.float32)
    short_rows = short((rows, width))
    before = got("pk")[:, kv_rows : kv_rows + 2, 0].astype(jnp.int32)
    before = before[:, :1] * DIGIT + before[:, 1:]
    database_blocks = [a for place in range(blocks) for a in (database_at(place), swapped_at(place))]
    values, normed = call(
        functools.partial(gather_kernel, blocks),
        (short_rows, short_rows),
        "ssss" + "v" * (1 + 2 * blocks),
        "neighbour_rows",
        10 * rows * width,
        16 + (8 * blocks * database_half.size >> 20),
    )(ready("gather", here), host, index, before, enc_gain, *database_blocks)

    def attention(so_far, weights, kv, far):
        return call(
            functools.partial(attention_kernel, len(kv), far),
            long_rows,
            "svv" + "v" * 3 * len(kv),
            "encoder_attention",
            gemm * 2 * len(kv) // lanes,
            24,
        )(here, so_far, normed, *weights, *kv)

    arrived["near"] = attention(
        ready("near", values), (query_t, enc_out, *got("ca")), (got("keys"), got("ck")), False
    )
    far_weights = (got("ya"), got("xa"), got("cya"), got("cxa"))
    resid = attention(got("near"), far_weights, (got("yk"), got("cyk")), True)
    arrived["far"] = resid

    near_units = (up_t, ffn_down, *got("cf"))
    partial_rows, normed = call(
        functools.partial(ffn_kernel, False, True),
        (long_rows, short_rows),
        "vv" + "v" * len(near_units),
        "encoder_ffn_near",
        2 * gemm,
        30,
    )(ffn_gain, resid, *near_units)
    arrived["units"] = partial_rows
    far_units = [got(name) for name in ("yf", "cyf", "zf", "czf")]
    encoded = call(
        functools.partial(ffn_kernel, True, False),
        short_rows,
        "vvv" + "v" * len(far_units),
        "encoder_ffn_far",
        2 * gemm,
        30,
        scratch=[pltpu.VMEM((rows, width), jnp.float32)],
    )(ffn_gain, partial_rows, normed, *far_units)

    other = core_swap(encoded)
    pairs_shape = (rows, 2 * dec_width)
    pairs_flops = 2 * rows * width * 2 * dec_width
    own_pairs = call(
        pairs_kernel,
        jax.ShapeDtypeStruct(pairs_shape, jnp.bfloat16),
        "vv",
        "decoder_pairs",
        pairs_flops,
        20,
    )(encoded, got("wk"))
    return call(
        decoder_kernel,
        jax.ShapeDtypeStruct(dec_queries.shape, jnp.float32),
        "svvvv",
        "decoder_attention",
        pairs_flops,
        28,
        scratch=[pltpu.VMEM(pairs_shape, jnp.bfloat16)],
    )(here, own_pairs, other, got("wk"), dec_queries)


def solution(mesh):
    placed = (
        P("seq", None, "mp"),
        P("seq", "mp"),
        P("seq", None, None),
        P("seq", None),
        P("seq", None),
        P(),
        P(None, "mp"),
        P("mp", None),
        P(),
        P(None, "mp"),
        P("mp", None),
        P(None, None, "mp"),
    )
    return jax.shard_map(
        on_device, mesh=mesh, in_specs=placed, out_specs=P("seq", "mp"), check_vma=False
    )
```

```python
import functools

import jax
import jax.numpy as jnp
from jax import lax
from jax.experimental import pallas as pl
from jax.experimental.pallas import tpu as pltpu
from jax.sharding import PartitionSpec as P

HEAD_DIM = 128
EHEAD_DIM = 112
SPAN = 64
NBL = 128
NEIGH = 2
CH_DEV = 8
HALVES = 2
BLOCK = 512
DIGIT = 128

ORDER = {
    "pk": ("x0",),
    "xp": ("xn",),
    "xa": ("xm",),
    "ca": ("xn",),
    "cf": ("xn",),
    "keys": ("xp",),
    "yk": ("yf", "xm",),
    "cya": ("yf",),
    "cyf": ("far",),
    "cyk": ("near",),
    "czf": ("far",),
    "near": ("yf",),
    "wk": ("ya",),
    "gains": ("zn",),
}

NT = (((1,), (1,)), ((), ()))
NN = (((1,), (0,)), ((), ()))


def mxu(lhs, rhs, dims):
    return lax.dot_general(lhs, rhs, dims, preferred_element_type=jnp.float32)


def rms_scale(values, gain):
    return values * lax.rsqrt(jnp.mean(values * values, axis=-1, keepdims=True) + 1e-06) * gain


def turned(chunk):
    return jnp.concatenate([chunk[:, SPAN:], chunk[:, :SPAN]], axis=1)


def prepare_kernel(here, lane_here, host, index, database, query_t, enc_out, up_t, down, kv_t, *refs):
    db_half, attention_half, ffn_half, packet = refs[:4]
    db_in, db_out, kv_in, packet_out, attention_out, ffn_out, sems = refs[4:]
    per_host, half_rows, width = db_half.shape
    seq, lane = here[0], lane_here[0]
    copies = [
        pltpu.make_async_copy(
            database.at[:, pl.ds(pl.multiple_of(lane % HALVES * half_rows, half_rows), half_rows)],
            db_in,
            sems.at[0],
        ),
        pltpu.make_async_copy(kv_t.at[:, :, pl.ds(kv_t.shape[2] - 2 * SPAN, 2 * SPAN)], kv_in, sems.at[1]),
    ]
    halves = ((up_t, ffn_out, 0, seq // 2 % 2), (down, ffn_out, 1, seq // 2 % 2))
    halves += ((query_t, attention_out, 0, seq % 2), (enc_out, attention_out, 1, seq % 2))
    for i, (source, target, spot, parity) in enumerate(halves):
        count = source.shape[0] // 2
        copies.append(
            pltpu.make_async_copy(
                source.at[pl.ds(pl.multiple_of(parity * count, 16), count)],
                target.at[pl.ds(spot * count, count)],
                sems.at[2 + i],
            )
        )
    for copy in copies:
        copy.start()
    backs = []

    def back(source, target):
        backs.append(pltpu.make_async_copy(source, target, sems.at[6 + len(backs)]))
        backs[-1].start()

    copies[0].wait()
    db_out[...] = db_in[...].astype(jnp.bfloat16)
    back(db_out, db_half)
    copies[1].wait()
    kv_rows = kv_in.shape[1]
    row = lax.broadcasted_iota(jnp.int32, (packet.shape[1] - kv_rows, SPAN), 0)
    for k in range(NEIGH):
        entry = host[k, CH_DEV - 1] * per_host + index[k, CH_DEV - 1]
        digits = jnp.where(row == 0, entry // DIGIT, jnp.where(row == 1, entry % DIGIT, 0))
        packet_out[k, :kv_rows, :] = kv_in[k][:, SPAN:]
        packet_out[k, kv_rows:, :] = digits.astype(jnp.float32).astype(jnp.bfloat16)
    back(packet_out, packet)
    for copy in copies[2:4]:
        copy.wait()
    back(ffn_out, ffn_half)
    for copy in copies[4:]:
        copy.wait()
    back(attention_out, attention_half)
    for copy in backs:
        copy.wait()


def gather_kernel(blocks, here, host, index, before, gain, *refs):
    *db_refs, rows_out, normed_out = refs
    per_host, part_rows, width = db_refs[0].shape
    seq = here[0]
    for i in range(CH_DEV * NEIGH):
        span, k = i // NEIGH, i % NEIGH
        if span == 0:
            of_host, place = before[k, 0] // per_host, before[k, 0] % per_host
        else:
            of_host, place = host[k, span - 1], index[k, span - 1]
        block = (seq // 2 - of_host // 2 + blocks) % blocks * 2 + (seq + of_host) % 2
        for b in range(2 * blocks):

            @pl.when(block == b)
            def _(b=b, place=place, i=i):
                rows_out[i * part_rows : (i + 1) * part_rows, :] = db_refs[b][place]

    values = rows_out[...].astype(jnp.float32)
    normed_out[...] = rms_scale(values, gain[...]).astype(jnp.bfloat16)


def attention_kernel(pieces, far, seq_index, before, normed_in, *refs):
    weight_refs, kv_refs, (result,) = refs[: 2 * pieces], refs[2 * pieces : 3 * pieces], refs[3 * pieces :]
    rows, width = before.shape
    span_rows = rows // CH_DEV
    pair_rows = 2 * span_rows
    pad = HEAD_DIM - EHEAD_DIM
    scale = float(EHEAD_DIM) ** (-0.5)
    odd = seq_index[0] % 2
    lane = lax.broadcasted_iota(jnp.int32, (pair_rows, 2 * SPAN), 1)
    row = lax.broadcasted_iota(jnp.int32, (pair_rows, 2 * SPAN), 0)
    own_lanes = (lane < SPAN) == (row < span_rows)
    rest = jnp.zeros((pad, 2 * SPAN), jnp.bfloat16)
    empty = jnp.zeros((HEAD_DIM, 2 * SPAN), jnp.bfloat16)
    ones = jnp.ones((2 * HEAD_DIM - EHEAD_DIM, 2 * SPAN), jnp.bfloat16)
    weight_rest = jnp.zeros((pad, width), jnp.bfloat16)
    q_parts, out_parts = [], []
    for p in range(pieces):
        first, second = weight_refs[2 * p][...], weight_refs[2 * p + 1][...]
        if far:
            first, second = (
                jnp.where(odd == 0, first, second),
                jnp.where(odd == 0, second, first),
            )
            q_parts += [first[:EHEAD_DIM], weight_rest, second[:EHEAD_DIM], weight_rest]
            out_parts += [first[EHEAD_DIM:], weight_rest, second[EHEAD_DIM:], weight_rest]
        else:
            q_parts += [first[:EHEAD_DIM], weight_rest, first[EHEAD_DIM:], weight_rest]
            out_parts += [second[:EHEAD_DIM], weight_rest, second[EHEAD_DIM:], weight_rest]
    q_w, out_w = jnp.concatenate(q_parts, axis=0), jnp.concatenate(out_parts, axis=0)
    left = lax.broadcasted_iota(jnp.int32, (BLOCK, 2 * SPAN), 1) < SPAN
    for start in range(0, rows, BLOCK):
        block = slice(start, start + BLOCK)
        query = (mxu(normed_in[block, :], q_w, NT) * scale).astype(jnp.bfloat16)
        attended = []
        for p in range(pieces):
            scores = []
            for at in range(0, BLOCK, pair_rows):
                tok = (start + at) // pair_rows * 2 * SPAN
                keys = kv_refs[p][0, :, tok : tok + 2 * SPAN]
                keys = jnp.concatenate(
                    [
                        jnp.concatenate([keys[:EHEAD_DIM], rest, empty], axis=0),
                        jnp.concatenate([empty, turned(keys[EHEAD_DIM:]), rest], axis=0),
                    ],
                    axis=1,
                )
                of_piece = query[at : at + pair_rows, 2 * HEAD_DIM * p : 2 * HEAD_DIM * (p + 1)]
                both = mxu(of_piece, keys, NN)
                scores.append(jnp.where(own_lanes, both[:, : 2 * SPAN], both[:, 2 * SPAN :]))
            scores = jnp.concatenate(scores, axis=0)
            low = jnp.max(jnp.where(left, scores, -jnp.inf), axis=1, keepdims=True)
            high = jnp.max(jnp.where(left, -jnp.inf, scores), axis=1, keepdims=True)
            weights = jnp.exp(scores - jnp.where(left, low, high)).astype(jnp.bfloat16)
            of_heads = [[], []]
            for at in range(0, BLOCK, pair_rows):
                tok = (start + at) // pair_rows * 2 * SPAN
                part = weights[at : at + pair_rows]
                vals = kv_refs[p][1, :, tok : tok + 2 * SPAN]
                for head in range(2):
                    picked = jnp.where(own_lanes if head == 0 else ~own_lanes, part, jnp.zeros_like(part))
                    of_head = vals[:EHEAD_DIM] if head == 0 else turned(vals[EHEAD_DIM:])
                    mixed = mxu(picked, jnp.concatenate([of_head, ones], axis=0), NT)
                    of_heads[head].append((mixed[:, :HEAD_DIM] / mixed[:, HEAD_DIM:]).astype(jnp.bfloat16))
            attended += [jnp.concatenate(parts, axis=0) for parts in of_heads]
        added = mxu(jnp.concatenate(attended, axis=1), out_w, NN)
        result[block, :] = before[block, :].astype(jnp.float32) + added


def ffn_kernel(far, first, gain, before, *refs):
    if first:
        *group_refs, result, normed = refs
    else:
        normed, *group_refs, result = refs
    if far:
        half = group_refs[0].shape[0] // 2
        ups, downs = [r[:half] for r in group_refs], [r[half:] for r in group_refs]
    else:
        ups, downs = [r[...] for r in group_refs[::2]], [r[...] for r in group_refs[1::2]]
    up, down = jnp.concatenate(ups, axis=0), jnp.concatenate(downs, axis=0)
    raised = []
    for start in range(0, before.shape[0], BLOCK):
        block = slice(start, start + BLOCK)
        if first:
            normed[block, :] = rms_scale(before[block, :], gain[...]).astype(jnp.bfloat16)
        raised.append(mxu(normed[block, :], up, NT).astype(jnp.bfloat16))
    for i, units in enumerate(raised):
        block = slice(i * BLOCK, (i + 1) * BLOCK)
        added = before[block, :] + mxu(jax.nn.gelu(units), down, NN)
        result[block, :] = added.astype(result.dtype)


def pairs_kernel(encoded, weights, pairs):
    pairs[...] = mxu(encoded[...], weights[...], NN).astype(jnp.bfloat16)


def decoder_kernel(first, own_pairs, other, weights, queries, out, other_pairs):
    rows = other.shape[0]
    part = rows // CH_DEV
    width = queries.shape[1]
    scale = float(HEAD_DIM) ** (-0.5)
    other_pairs[...] = mxu(other[...], weights[...], NN).astype(jnp.bfloat16)

    def span_pairs_of(span, col):
        return jnp.concatenate(
            [r[span * part : (span + 1) * part, col : col + HEAD_DIM] for r in (own_pairs, other_pairs)],
            axis=0,
        )

    ones = jnp.ones((2 * part, HEAD_DIM), jnp.bfloat16)
    for head in range(width // HEAD_DIM):
        col = head * HEAD_DIM
        query = (queries[:, col : col + HEAD_DIM].astype(jnp.float32) * scale).astype(jnp.bfloat16)
        scores = jnp.concatenate(
            [
                mxu(query[span * SPAN : (span + 1) * SPAN], span_pairs_of(span, col), NT)
                for span in range(CH_DEV)
            ],
            axis=0,
        )
        weights_b = jnp.exp(scores - jnp.max(scores, axis=1, keepdims=True)).astype(jnp.bfloat16)
        for span in range(CH_DEV):
            vals = jnp.concatenate([span_pairs_of(span, width + col), ones], axis=1)
            result = mxu(weights_b[span * SPAN : (span + 1) * SPAN], vals, NN)
            result = result[:, :HEAD_DIM] / result[:, HEAD_DIM:]
            if span == 0:
                result = jnp.where(first[0] == 0, jnp.zeros_like(result), result)
            out[span * SPAN : (span + 1) * SPAN, col : col + HEAD_DIM] = result


def call(body, out_shape, in_specs, name, flops, vmem_mib, scratch=(), out="v"):
    spaces = {"s": pltpu.SMEM, "v": pltpu.VMEM, "h": pl.ANY}
    return pl.pallas_call(
        body,
        out_shape=out_shape,
        in_specs=[pl.BlockSpec(memory_space=spaces[c]) for c in in_specs],
        out_specs=jax.tree.map(lambda _: pl.BlockSpec(memory_space=spaces[out]), out_shape),
        scratch_shapes=list(scratch),
        compiler_params=pltpu.CompilerParams(vmem_limit_bytes=vmem_mib * 1024 * 1024),
        cost_estimate=pl.CostEstimate(flops=flops, bytes_accessed=8_000_000, transcendentals=0),
        name=name,
    )


def on_device(
    span_pairs,
    dec_queries,
    database,
    nbr_index,
    nbr_host,
    enc_gain,
    enc_query,
    enc_out,
    ffn_gain,
    ffn_up,
    ffn_down,
    dec_kv,
):
    seq_size = lax.axis_size("seq")
    lanes = lax.axis_size("mp")
    seq_index = lax.axis_index("seq")
    lane_index = lax.axis_index("mp")
    entries_here, block_rows, width = database.shape
    half_rows = block_rows // HALVES
    rows = CH_DEV * NEIGH * half_rows
    blocks = seq_size // 2

    def core_swap(array):
        return lax.ppermute(array, "mp", [(i, i ^ 1) for i in range(lanes)])

    def lane_step(array, step):
        return lax.ppermute(array, "mp", [(i, (i + 2 * step) % lanes) for i in range(lanes)])

    def seq_swap(array):
        return lax.ppermute(array, "seq", [(i, i ^ 1) for i in range(seq_size)])

    def seq_cross(array):
        return lax.ppermute(array, "seq", [(i, i ^ 2) for i in range(seq_size)])

    def seq_ring(array, way):
        return lax.ppermute(array, "seq", [(i, (i + 2 * way) % seq_size) for i in range(seq_size)])

    def next_seq(array):
        return lax.ppermute(array, "seq", [(i, i + 1) for i in range(seq_size - 1)])

    query_t, up_t = enc_query.T, ffn_up.T
    kv_t = jnp.transpose(span_pairs, (1, 2, 0))
    kv_rows, tokens = kv_t.shape[1:]
    kept = tokens - SPAN

    here = seq_index.reshape(1).astype(jnp.int32)
    lane_here = lane_index.reshape(1).astype(jnp.int32)
    host, index = nbr_host.T, nbr_index.T
    dma = pltpu.SemaphoreType.DMA
    short = functools.partial(jax.ShapeDtypeStruct, dtype=jnp.bfloat16)
    database_half, attention_half, ffn_half, packet = call(
        prepare_kernel,
        (
            short((entries_here, half_rows, width)),
            short(enc_out.shape),
            short(ffn_down.shape),
            short((2, kv_rows + 16, SPAN)),
        ),
        "ssss" + "h" * 6,
        "prepare",
        rows * width,
        60,
        scratch=[
            pltpu.VMEM((entries_here, half_rows, width), jnp.float32),
            pltpu.VMEM((entries_here, half_rows, width), jnp.bfloat16),
            pltpu.VMEM((2, kv_rows, 2 * SPAN), jnp.bfloat16),
            pltpu.VMEM((2, kv_rows + 16, SPAN), jnp.bfloat16),
            pltpu.VMEM(enc_out.shape, jnp.bfloat16),
            pltpu.VMEM(ffn_down.shape, jnp.bfloat16),
            dma((10,)),
        ],
        out="h",
    )(here, lane_here, host, index, database, query_t, enc_out, up_t, ffn_down, kv_t)

    dec_width = dec_kv.shape[2]
    middle, last = blocks // 2, blocks - 1
    names = {"0": 0, "n": 1, "p": last, "m": middle}
    short_name = {place: name for name, place in names.items()}
    arrived = {}

    def got(name):
        if name not in arrived:
            arrived[name] = makers[name]()
        return arrived[name]

    def ready(name, array):
        others = [got(other) for other in ORDER.get(name, ())]
        return lax.optimization_barrier((array, others))[0] if others else array

    def database(place):
        if place == 0:
            return database_half
        way = 1 if place <= middle else -1
        source = database_at((place - way) % blocks)
        return seq_ring(ready(f"z{short_name.get(place, place)}", source), way)

    def database_at(place):
        return got(f"z{short_name.get(place, place)}")

    def swapped_at(place):
        return got(f"x{short_name.get(place, place)}")

    def received_keys():
        return jnp.concatenate([got("pk")[:, :kv_rows], kv_t[:, :, :kept]], axis=2)

    def both_cores(name, arrays):
        return tuple(core_swap(a) for a in ready(name, arrays))

    makers = {
        "ya": lambda: lane_step(ready("ya", attention_half), 1),
        "yf": lambda: lane_step(ready("yf", ffn_half), 1),
        "yk": lambda: lane_step(ready("yk", got("keys")), 1),
        "pk": lambda: next_seq(ready("pk", packet)),
        "keys": lambda: ready("keys", received_keys()),
        "xa": lambda: seq_swap(ready("xa", got("ya"))),
        "zf": lambda: seq_cross(ready("zf", got("yf"))),
        "ca": lambda: both_cores("ca", (query_t, enc_out)),
        "cf": lambda: both_cores("cf", (up_t, ffn_down)),
        "ck": lambda: core_swap(ready("ck", got("keys"))),
        "cya": lambda: core_swap(ready("cya", got("ya"))),
        "cyk": lambda: core_swap(ready("cyk", got("yk"))),
        "cyf": lambda: core_swap(ready("cyf", got("yf"))),
        "cxa": lambda: core_swap(ready("cxa", got("xa"))),
        "czf": lambda: core_swap(ready("czf", got("zf"))),
        "wk": lambda: ready("wk", dec_kv.reshape(width, 2 * dec_width)),
    }
    for place in range(blocks):
        name = short_name.get(place, place)
        makers[f"z{name}"] = functools.partial(database, place)
        makers[f"x{name}"] = lambda place=place, name=name: seq_swap(ready(f"x{name}", database_at(place)))
    enc_gain, ffn_gain = enc_gain.reshape(1, width), ffn_gain.reshape(1, width)
    enc_gain, ffn_gain = ready("gains", (enc_gain, ffn_gain))

    gemm = 2 * rows * width * width
    long_rows = jax.ShapeDtypeStruct((rows, width), jnp.float32)
    short_rows = short((rows, width))
    before = got("pk")[:, kv_rows : kv_rows + 2, 0].astype(jnp.int32)
    before = before[:, :1] * DIGIT + before[:, 1:]
    database_blocks = [a for place in range(blocks) for a in (database_at(place), swapped_at(place))]
    values, normed = call(
        functools.partial(gather_kernel, blocks),
        (short_rows, short_rows),
        "ssss" + "v" * (1 + 2 * blocks),
        "neighbour_rows",
        10 * rows * width,
        16 + (8 * blocks * database_half.size >> 20),
    )(ready("gather", here), host, index, before, enc_gain, *database_blocks)

    def attention(so_far, weights, kv, far):
        return call(
            functools.partial(attention_kernel, len(kv), far),
            long_rows,
            "svv" + "v" * 3 * len(kv),
            "encoder_attention",
            gemm * 2 * len(kv) // lanes,
            24,
        )(here, so_far, normed, *weights, *kv)

    arrived["near"] = attention(
        ready("near", values), (query_t, enc_out, *got("ca")), (got("keys"), got("ck")), False
    )
    far_weights = (got("ya"), got("xa"), got("cya"), got("cxa"))
    resid = attention(got("near"), far_weights, (got("yk"), got("cyk")), True)
    arrived["far"] = resid

    near_units = (up_t, ffn_down, *got("cf"))
    partial_rows, normed = call(
        functools.partial(ffn_kernel, False, True),
        (long_rows, short_rows),
        "vv" + "v" * len(near_units),
        "encoder_ffn_near",
        2 * gemm,
        30,
    )(ffn_gain, resid, *near_units)
    arrived["units"] = partial_rows
    far_units = [got(name) for name in ("yf", "cyf", "zf", "czf")]
    encoded = call(
        functools.partial(ffn_kernel, True, False),
        short_rows,
        "vvv" + "v" * len(far_units),
        "encoder_ffn_far",
        2 * gemm,
        30,
    )(ffn_gain, partial_rows, normed, *far_units)

    other = core_swap(encoded)
    pairs_shape = (rows, 2 * dec_width)
    pairs_flops = 2 * rows * width * 2 * dec_width
    own_pairs = call(
        pairs_kernel,
        jax.ShapeDtypeStruct(pairs_shape, jnp.bfloat16),
        "vv",
        "decoder_pairs",
        pairs_flops,
        20,
    )(encoded, got("wk"))
    return call(
        decoder_kernel,
        jax.ShapeDtypeStruct(dec_queries.shape, jnp.float32),
        "svvvv",
        "decoder_attention",
        pairs_flops,
        28,
        scratch=[pltpu.VMEM(pairs_shape, jnp.bfloat16)],
    )(here, own_pairs, other, got("wk"), dec_queries)


def solution(mesh):
    placed = (
        P("seq", None, "mp"),
        P("seq", "mp"),
        P("seq", None, None),
        P("seq", None),
        P("seq", None),
        P(),
        P(None, "mp"),
        P("mp", None),
        P(),
        P(None, "mp"),
        P("mp", None),
        P(None, None, "mp"),
    )
    return jax.shard_map(
        on_device, mesh=mesh, in_specs=placed, out_specs=P("seq", "mp"), check_vma=False
    )
```

```python
import functools

import jax
import jax.numpy as jnp
from jax import lax
from jax.experimental import pallas as pl
from jax.experimental.pallas import tpu as pltpu
from jax.sharding import PartitionSpec as P

HEAD_DIM = 128
EHEAD_DIM = 112
SPAN = 64
NBL = 128
NEIGH = 2
CH_DEV = 8
HALVES = 2
BLOCK = 512
DIGIT = 128

ORDER = {
    "pk": ("x0",),
    "xp": ("xn",),
    "xa": ("xm",),
    "ca": ("xn",),
    "cf": ("xn",),
    "keys": ("xp",),
    "yk": ("yf", "xm",),
    "cya": ("yf",),
    "cyf": ("far",),
    "cyk": ("near",),
    "czf": ("far",),
    "near": ("yf", "wk"),
    "wk": ("ya",),
    "gains": ("zn",),
}

NT = (((1,), (1,)), ((), ()))
NN = (((1,), (0,)), ((), ()))


def mxu(lhs, rhs, dims):
    return lax.dot_general(lhs, rhs, dims, preferred_element_type=jnp.float32)


def rms_scale(values, gain):
    return values * lax.rsqrt(jnp.mean(values * values, axis=-1, keepdims=True) + 1e-06) * gain


def turned(chunk):
    return jnp.concatenate([chunk[:, SPAN:], chunk[:, :SPAN]], axis=1)


def prepare_kernel(here, lane_here, host, index, database, query_t, enc_out, up_t, down, kv_t, *refs):
    db_half, attention_half, ffn_half, packet = refs[:4]
    db_in, db_out, kv_in, packet_out, attention_out, ffn_out, sems = refs[4:]
    per_host, half_rows, width = db_half.shape
    seq, lane = here[0], lane_here[0]
    copies = [
        pltpu.make_async_copy(
            database.at[:, pl.ds(pl.multiple_of(lane % HALVES * half_rows, half_rows), half_rows)],
            db_in,
            sems.at[0],
        ),
        pltpu.make_async_copy(kv_t.at[:, :, pl.ds(kv_t.shape[2] - 2 * SPAN, 2 * SPAN)], kv_in, sems.at[1]),
    ]
    halves = ((up_t, ffn_out, 0, seq // 2 % 2), (down, ffn_out, 1, seq // 2 % 2))
    halves += ((query_t, attention_out, 0, seq % 2), (enc_out, attention_out, 1, seq % 2))
    for i, (source, target, spot, parity) in enumerate(halves):
        count = source.shape[0] // 2
        copies.append(
            pltpu.make_async_copy(
                source.at[pl.ds(pl.multiple_of(parity * count, 16), count)],
                target.at[pl.ds(spot * count, count)],
                sems.at[2 + i],
            )
        )
    for copy in copies:
        copy.start()
    backs = []

    def back(source, target):
        backs.append(pltpu.make_async_copy(source, target, sems.at[6 + len(backs)]))
        backs[-1].start()

    copies[0].wait()
    db_out[...] = db_in[...].astype(jnp.bfloat16)
    back(db_out, db_half)
    copies[1].wait()
    kv_rows = kv_in.shape[1]
    row = lax.broadcasted_iota(jnp.int32, (packet.shape[1] - kv_rows, SPAN), 0)
    for k in range(NEIGH):
        entry = host[k, CH_DEV - 1] * per_host + index[k, CH_DEV - 1]
        digits = jnp.where(row == 0, entry // DIGIT, jnp.where(row == 1, entry % DIGIT, 0))
        packet_out[k, :kv_rows, :] = kv_in[k][:, SPAN:]
        packet_out[k, kv_rows:, :] = digits.astype(jnp.float32).astype(jnp.bfloat16)
    back(packet_out, packet)
    for copy in copies[2:4]:
        copy.wait()
    back(ffn_out, ffn_half)
    for copy in copies[4:]:
        copy.wait()
    back(attention_out, attention_half)
    for copy in backs:
        copy.wait()


def gather_kernel(blocks, here, host, index, before, gain, *refs):
    *db_refs, rows_out, normed_out = refs
    per_host, part_rows, width = db_refs[0].shape
    seq = here[0]
    for i in range(CH_DEV * NEIGH):
        span, k = i // NEIGH, i % NEIGH
        if span == 0:
            of_host, place = before[k, 0] // per_host, before[k, 0] % per_host
        else:
            of_host, place = host[k, span - 1], index[k, span - 1]
        block = (seq // 2 - of_host // 2 + blocks) % blocks * 2 + (seq + of_host) % 2
        for b in range(2 * blocks):

            @pl.when(block == b)
            def _(b=b, place=place, i=i):
                rows_out[i * part_rows : (i + 1) * part_rows, :] = db_refs[b][place]

    values = rows_out[...].astype(jnp.float32)
    normed_out[...] = rms_scale(values, gain[...]).astype(jnp.bfloat16)


def attention_kernel(pieces, far, seq_index, before, normed_in, *refs):
    weight_refs, kv_refs, (result,) = refs[: 2 * pieces], refs[2 * pieces : 3 * pieces], refs[3 * pieces :]
    rows, width = before.shape
    span_rows = rows // CH_DEV
    pair_rows = 2 * span_rows
    pad = HEAD_DIM - EHEAD_DIM
    scale = float(EHEAD_DIM) ** (-0.5)
    odd = seq_index[0] % 2
    lane = lax.broadcasted_iota(jnp.int32, (pair_rows, 2 * SPAN), 1)
    row = lax.broadcasted_iota(jnp.int32, (pair_rows, 2 * SPAN), 0)
    own_lanes = (lane < SPAN) == (row < span_rows)
    rest = jnp.zeros((pad, 2 * SPAN), jnp.bfloat16)
    empty = jnp.zeros((HEAD_DIM, 2 * SPAN), jnp.bfloat16)
    ones = jnp.ones((2 * HEAD_DIM - EHEAD_DIM, 2 * SPAN), jnp.bfloat16)
    weight_rest = jnp.zeros((pad, width), jnp.bfloat16)
    q_parts, out_parts = [], []
    for p in range(pieces):
        first, second = weight_refs[2 * p][...], weight_refs[2 * p + 1][...]
        if far:
            first, second = (
                jnp.where(odd == 0, first, second),
                jnp.where(odd == 0, second, first),
            )
            q_parts += [first[:EHEAD_DIM], weight_rest, second[:EHEAD_DIM], weight_rest]
            out_parts += [first[EHEAD_DIM:], weight_rest, second[EHEAD_DIM:], weight_rest]
        else:
            q_parts += [first[:EHEAD_DIM], weight_rest, first[EHEAD_DIM:], weight_rest]
            out_parts += [second[:EHEAD_DIM], weight_rest, second[EHEAD_DIM:], weight_rest]
    q_w, out_w = jnp.concatenate(q_parts, axis=0), jnp.concatenate(out_parts, axis=0)
    left = lax.broadcasted_iota(jnp.int32, (BLOCK, 2 * SPAN), 1) < SPAN
    for start in range(0, rows, BLOCK):
        block = slice(start, start + BLOCK)
        query = (mxu(normed_in[block, :], q_w, NT) * scale).astype(jnp.bfloat16)
        attended = []
        for p in range(pieces):
            scores = []
            for at in range(0, BLOCK, pair_rows):
                tok = (start + at) // pair_rows * 2 * SPAN
                keys = kv_refs[p][0, :, tok : tok + 2 * SPAN]
                keys = jnp.concatenate(
                    [
                        jnp.concatenate([keys[:EHEAD_DIM], rest, empty], axis=0),
                        jnp.concatenate([empty, turned(keys[EHEAD_DIM:]), rest], axis=0),
                    ],
                    axis=1,
                )
                of_piece = query[at : at + pair_rows, 2 * HEAD_DIM * p : 2 * HEAD_DIM * (p + 1)]
                both = mxu(of_piece, keys, NN)
                scores.append(jnp.where(own_lanes, both[:, : 2 * SPAN], both[:, 2 * SPAN :]))
            scores = jnp.concatenate(scores, axis=0)
            low = jnp.max(jnp.where(left, scores, -jnp.inf), axis=1, keepdims=True)
            high = jnp.max(jnp.where(left, -jnp.inf, scores), axis=1, keepdims=True)
            weights = jnp.exp(scores - jnp.where(left, low, high)).astype(jnp.bfloat16)
            of_heads = [[], []]
            for at in range(0, BLOCK, pair_rows):
                tok = (start + at) // pair_rows * 2 * SPAN
                part = weights[at : at + pair_rows]
                vals = kv_refs[p][1, :, tok : tok + 2 * SPAN]
                for head in range(2):
                    picked = jnp.where(own_lanes if head == 0 else ~own_lanes, part, jnp.zeros_like(part))
                    of_head = vals[:EHEAD_DIM] if head == 0 else turned(vals[EHEAD_DIM:])
                    mixed = mxu(picked, jnp.concatenate([of_head, ones], axis=0), NT)
                    of_heads[head].append((mixed[:, :HEAD_DIM] / mixed[:, HEAD_DIM:]).astype(jnp.bfloat16))
            attended += [jnp.concatenate(parts, axis=0) for parts in of_heads]
        added = mxu(jnp.concatenate(attended, axis=1), out_w, NN)
        result[block, :] = before[block, :].astype(jnp.float32) + added


def ffn_kernel(far, first, gain, before, *refs):
    if first:
        *group_refs, result, normed = refs
    else:
        normed, *group_refs, result = refs
    if far:
        half = group_refs[0].shape[0] // 2
        ups, downs = [r[:half] for r in group_refs], [r[half:] for r in group_refs]
    else:
        ups, downs = [r[...] for r in group_refs[::2]], [r[...] for r in group_refs[1::2]]
    up, down = jnp.concatenate(ups, axis=0), jnp.concatenate(downs, axis=0)
    raised = []
    for start in range(0, before.shape[0], BLOCK):
        block = slice(start, start + BLOCK)
        if first:
            normed[block, :] = rms_scale(before[block, :], gain[...]).astype(jnp.bfloat16)
        raised.append(mxu(normed[block, :], up, NT).astype(jnp.bfloat16))
    for i, units in enumerate(raised):
        block = slice(i * BLOCK, (i + 1) * BLOCK)
        added = before[block, :] + mxu(jax.nn.gelu(units), down, NN)
        result[block, :] = added.astype(result.dtype)


def pairs_kernel(encoded, weights, pairs):
    pairs[...] = mxu(encoded[...], weights[...], NN).astype(jnp.bfloat16)


def decoder_kernel(first, own_pairs, other, weights, queries, out, other_pairs, held, sems):
    rows = other.shape[0]
    part = rows // CH_DEV
    width = queries.shape[1]
    scale = float(HEAD_DIM) ** (-0.5)
    other_pairs[...] = mxu(other[...], weights[...], NN).astype(jnp.bfloat16)

    def span_pairs_of(span, col):
        return jnp.concatenate(
            [r[span * part : (span + 1) * part, col : col + HEAD_DIM] for r in (own_pairs, other_pairs)],
            axis=0,
        )

    ones = jnp.ones((2 * part, HEAD_DIM), jnp.bfloat16)
    copies = []
    for head in range(width // HEAD_DIM):
        col = head * HEAD_DIM
        query = (queries[:, col : col + HEAD_DIM].astype(jnp.float32) * scale).astype(jnp.bfloat16)
        scores = jnp.concatenate(
            [
                mxu(query[span * SPAN : (span + 1) * SPAN], span_pairs_of(span, col), NT)
                for span in range(CH_DEV)
            ],
            axis=0,
        )
        weights_b = jnp.exp(scores - jnp.max(scores, axis=1, keepdims=True)).astype(jnp.bfloat16)
        for span in range(CH_DEV):
            vals = jnp.concatenate([span_pairs_of(span, width + col), ones], axis=1)
            result = mxu(weights_b[span * SPAN : (span + 1) * SPAN], vals, NN)
            result = result[:, :HEAD_DIM] / result[:, HEAD_DIM:]
            if span == 0:
                result = jnp.where(first[0] == 0, jnp.zeros_like(result), result)
            held[head, span * SPAN : (span + 1) * SPAN, :] = result
        copies.append(
            pltpu.make_async_copy(held.at[head], out.at[:, pl.ds(col, HEAD_DIM)], sems.at[head])
        )
        copies[-1].start()
    for copy in copies:
        copy.wait()


def call(body, out_shape, in_specs, name, flops, vmem_mib, scratch=(), out="v"):
    spaces = {"s": pltpu.SMEM, "v": pltpu.VMEM, "h": pl.ANY}
    return pl.pallas_call(
        body,
        out_shape=out_shape,
        in_specs=[pl.BlockSpec(memory_space=spaces[c]) for c in in_specs],
        out_specs=jax.tree.map(lambda _: pl.BlockSpec(memory_space=spaces[out]), out_shape),
        scratch_shapes=list(scratch),
        compiler_params=pltpu.CompilerParams(vmem_limit_bytes=vmem_mib * 1024 * 1024),
        cost_estimate=pl.CostEstimate(flops=flops, bytes_accessed=8_000_000, transcendentals=0),
        name=name,
    )


def on_device(
    span_pairs,
    dec_queries,
    database,
    nbr_index,
    nbr_host,
    enc_gain,
    enc_query,
    enc_out,
    ffn_gain,
    ffn_up,
    ffn_down,
    dec_kv,
):
    seq_size = lax.axis_size("seq")
    lanes = lax.axis_size("mp")
    seq_index = lax.axis_index("seq")
    lane_index = lax.axis_index("mp")
    entries_here, block_rows, width = database.shape
    half_rows = block_rows // HALVES
    rows = CH_DEV * NEIGH * half_rows
    blocks = seq_size // 2

    def core_swap(array):
        return lax.ppermute(array, "mp", [(i, i ^ 1) for i in range(lanes)])

    def lane_step(array, step):
        return lax.ppermute(array, "mp", [(i, (i + 2 * step) % lanes) for i in range(lanes)])

    def seq_swap(array):
        return lax.ppermute(array, "seq", [(i, i ^ 1) for i in range(seq_size)])

    def seq_cross(array):
        return lax.ppermute(array, "seq", [(i, i ^ 2) for i in range(seq_size)])

    def seq_ring(array, way):
        return lax.ppermute(array, "seq", [(i, (i + 2 * way) % seq_size) for i in range(seq_size)])

    def next_seq(array):
        return lax.ppermute(array, "seq", [(i, i + 1) for i in range(seq_size - 1)])

    query_t, up_t = enc_query.T, ffn_up.T
    kv_t = jnp.transpose(span_pairs, (1, 2, 0))
    kv_rows, tokens = kv_t.shape[1:]
    kept = tokens - SPAN

    here = seq_index.reshape(1).astype(jnp.int32)
    lane_here = lane_index.reshape(1).astype(jnp.int32)
    host, index = nbr_host.T, nbr_index.T
    dma = pltpu.SemaphoreType.DMA
    short = functools.partial(jax.ShapeDtypeStruct, dtype=jnp.bfloat16)
    database_half, attention_half, ffn_half, packet = call(
        prepare_kernel,
        (
            short((entries_here, half_rows, width)),
            short(enc_out.shape),
            short(ffn_down.shape),
            short((2, kv_rows + 16, SPAN)),
        ),
        "ssss" + "h" * 6,
        "prepare",
        rows * width,
        53,
        scratch=[
            pltpu.VMEM((entries_here, half_rows, width), jnp.float32),
            pltpu.VMEM((entries_here, half_rows, width), jnp.bfloat16),
            pltpu.VMEM((2, kv_rows, 2 * SPAN), jnp.bfloat16),
            pltpu.VMEM((2, kv_rows + 16, SPAN), jnp.bfloat16),
            pltpu.VMEM(enc_out.shape, jnp.bfloat16),
            pltpu.VMEM(ffn_down.shape, jnp.bfloat16),
            dma((10,)),
        ],
        out="h",
    )(here, lane_here, host, index, database, query_t, enc_out, up_t, ffn_down, kv_t)

    dec_width = dec_kv.shape[2]
    middle, last = blocks // 2, blocks - 1
    names = {"0": 0, "n": 1, "p": last, "m": middle}
    short_name = {place: name for name, place in names.items()}
    arrived = {}

    def got(name):
        if name not in arrived:
            arrived[name] = makers[name]()
        return arrived[name]

    def ready(name, array):
        others = [got(other) for other in ORDER.get(name, ())]
        return lax.optimization_barrier((array, others))[0] if others else array

    def database(place):
        if place == 0:
            return database_half
        way = 1 if place <= middle else -1
        source = database_at((place - way) % blocks)
        return seq_ring(ready(f"z{short_name.get(place, place)}", source), way)

    def database_at(place):
        return got(f"z{short_name.get(place, place)}")

    def swapped_at(place):
        return got(f"x{short_name.get(place, place)}")

    def received_keys():
        return jnp.concatenate([got("pk")[:, :kv_rows], kv_t[:, :, :kept]], axis=2)

    def both_cores(name, arrays):
        return tuple(core_swap(a) for a in ready(name, arrays))

    makers = {
        "ya": lambda: lane_step(ready("ya", attention_half), 1),
        "yf": lambda: lane_step(ready("yf", ffn_half), 1),
        "yk": lambda: lane_step(ready("yk", got("keys")), 1),
        "pk": lambda: next_seq(ready("pk", packet)),
        "keys": lambda: ready("keys", received_keys()),
        "xa": lambda: seq_swap(ready("xa", got("ya"))),
        "zf": lambda: seq_cross(ready("zf", got("yf"))),
        "ca": lambda: both_cores("ca", (query_t, enc_out)),
        "cf": lambda: both_cores("cf", (up_t, ffn_down)),
        "ck": lambda: core_swap(ready("ck", got("keys"))),
        "cya": lambda: core_swap(ready("cya", got("ya"))),
        "cyk": lambda: core_swap(ready("cyk", got("yk"))),
        "cyf": lambda: core_swap(ready("cyf", got("yf"))),
        "cxa": lambda: core_swap(ready("cxa", got("xa"))),
        "czf": lambda: core_swap(ready("czf", got("zf"))),
        "wk": lambda: ready("wk", dec_kv.reshape(width, 2 * dec_width)),
    }
    for place in range(blocks):
        name = short_name.get(place, place)
        makers[f"z{name}"] = functools.partial(database, place)
        makers[f"x{name}"] = lambda place=place, name=name: seq_swap(ready(f"x{name}", database_at(place)))
    enc_gain, ffn_gain = enc_gain.reshape(1, width), ffn_gain.reshape(1, width)
    enc_gain, ffn_gain = ready("gains", (enc_gain, ffn_gain))

    gemm = 2 * rows * width * width
    long_rows = jax.ShapeDtypeStruct((rows, width), jnp.float32)
    short_rows = short((rows, width))
    before = got("pk")[:, kv_rows : kv_rows + 2, 0].astype(jnp.int32)
    before = before[:, :1] * DIGIT + before[:, 1:]
    database_blocks = [a for place in range(blocks) for a in (database_at(place), swapped_at(place))]
    values, normed = call(
        functools.partial(gather_kernel, blocks),
        (short_rows, short_rows),
        "ssss" + "v" * (1 + 2 * blocks),
        "neighbour_rows",
        10 * rows * width,
        16 + (8 * blocks * database_half.size >> 20),
    )(ready("gather", here), host, index, before, enc_gain, *database_blocks)

    def attention(so_far, weights, kv, far):
        return call(
            functools.partial(attention_kernel, len(kv), far),
            long_rows,
            "svv" + "v" * 3 * len(kv),
            "encoder_attention",
            gemm * 2 * len(kv) // lanes,
            24,
        )(here, so_far, normed, *weights, *kv)

    arrived["near"] = attention(
        ready("near", values), (query_t, enc_out, *got("ca")), (got("keys"), got("ck")), False
    )
    far_weights = (got("ya"), got("xa"), got("cya"), got("cxa"))
    resid = attention(got("near"), far_weights, (got("yk"), got("cyk")), True)
    arrived["far"] = resid

    near_units = (up_t, ffn_down, *got("cf"))
    partial_rows, normed = call(
        functools.partial(ffn_kernel, False, True),
        (long_rows, short_rows),
        "vv" + "v" * len(near_units),
        "encoder_ffn_near",
        2 * gemm,
        30,
    )(ffn_gain, resid, *near_units)
    arrived["units"] = partial_rows
    far_units = [got(name) for name in ("yf", "cyf", "zf", "czf")]
    encoded = call(
        functools.partial(ffn_kernel, True, False),
        short_rows,
        "vvv" + "v" * len(far_units),
        "encoder_ffn_far",
        2 * gemm,
        30,
    )(ffn_gain, partial_rows, normed, *far_units)

    other = core_swap(encoded)
    pairs_shape = (rows, 2 * dec_width)
    pairs_flops = 2 * rows * width * 2 * dec_width
    own_pairs = call(
        pairs_kernel,
        jax.ShapeDtypeStruct(pairs_shape, jnp.bfloat16),
        "vv",
        "decoder_pairs",
        pairs_flops,
        20,
    )(encoded, got("wk"))
    return call(
        decoder_kernel,
        jax.ShapeDtypeStruct(dec_queries.shape, jnp.float32),
        "svvvv",
        "decoder_attention",
        pairs_flops,
        28,
        scratch=[
            pltpu.VMEM(pairs_shape, jnp.bfloat16),
            pltpu.VMEM((dec_width // HEAD_DIM, dec_queries.shape[0], HEAD_DIM), jnp.float32),
            dma((dec_width // HEAD_DIM,)),
        ],
        out="h",
    )(here, own_pairs, other, got("wk"), dec_queries)


def solution(mesh):
    placed = (
        P("seq", None, "mp"),
        P("seq", "mp"),
        P("seq", None, None),
        P("seq", None),
        P("seq", None),
        P(),
        P(None, "mp"),
        P("mp", None),
        P(),
        P(None, "mp"),
        P("mp", None),
        P(None, None, "mp"),
    )
    return jax.shard_map(
        on_device, mesh=mesh, in_specs=placed, out_specs=P("seq", "mp"), check_vma=False
    )
```

```python
import functools

import jax
import jax.numpy as jnp
from jax import lax
from jax.experimental import pallas as pl
from jax.experimental.pallas import tpu as pltpu
from jax.sharding import PartitionSpec as P

HEAD_DIM = 128
EHEAD_DIM = 112
SPAN = 64
NBL = 128
NEIGH = 2
CH_DEV = 8
HALVES = 2
BLOCK = 512
NORM_BLOCK = 64
DIGIT = 128

ORDER = {
    "pk": ("x0",),
    "xp": ("xn",),
    "xa": ("xm",),
    "ca": ("xn",),
    "cf": ("xn",),
    "keys": ("xp",),
    "yk": ("yf", "xm",),
    "cya": ("yf",),
    "cyf": ("far",),
    "cyk": ("near",),
    "czf": ("far",),
    "near": ("yf",),
    "wk": ("ya",),
    "gains": ("zn",),
}

NT = (((1,), (1,)), ((), ()))
NN = (((1,), (0,)), ((), ()))


def mxu(lhs, rhs, dims):
    return lax.dot_general(lhs, rhs, dims, preferred_element_type=jnp.float32)


def rms_scale(values, gain):
    return values * lax.rsqrt(jnp.mean(values * values, axis=-1, keepdims=True) + 1e-06) * gain


def turned(chunk):
    return jnp.concatenate([chunk[:, SPAN:], chunk[:, :SPAN]], axis=1)


def prepare_kernel(here, lane_here, host, index, database, query_t, enc_out, up_t, down, kv_t, *refs):
    db_half, attention_half, ffn_half, packet = refs[:4]
    db_in, db_out, kv_in, packet_out, attention_out, ffn_out, sems = refs[4:]
    per_host, half_rows, width = db_half.shape
    seq, lane = here[0], lane_here[0]
    copies = [
        pltpu.make_async_copy(
            database.at[:, pl.ds(pl.multiple_of(lane % HALVES * half_rows, half_rows), half_rows)],
            db_in,
            sems.at[0],
        ),
        pltpu.make_async_copy(kv_t.at[:, :, pl.ds(kv_t.shape[2] - 2 * SPAN, 2 * SPAN)], kv_in, sems.at[1]),
    ]
    halves = ((up_t, ffn_out, 0, seq // 2 % 2), (down, ffn_out, 1, seq // 2 % 2))
    halves += ((query_t, attention_out, 0, seq % 2), (enc_out, attention_out, 1, seq % 2))
    for i, (source, target, spot, parity) in enumerate(halves):
        count = source.shape[0] // 2
        copies.append(
            pltpu.make_async_copy(
                source.at[pl.ds(pl.multiple_of(parity * count, 16), count)],
                target.at[pl.ds(spot * count, count)],
                sems.at[2 + i],
            )
        )
    for copy in copies:
        copy.start()
    backs = []

    def back(source, target):
        backs.append(pltpu.make_async_copy(source, target, sems.at[6 + len(backs)]))
        backs[-1].start()

    copies[0].wait()
    db_out[...] = db_in[...].astype(jnp.bfloat16)
    back(db_out, db_half)
    copies[1].wait()
    kv_rows = kv_in.shape[1]
    row = lax.broadcasted_iota(jnp.int32, (packet.shape[1] - kv_rows, SPAN), 0)
    for k in range(NEIGH):
        entry = host[k, CH_DEV - 1] * per_host + index[k, CH_DEV - 1]
        digits = jnp.where(row == 0, entry // DIGIT, jnp.where(row == 1, entry % DIGIT, 0))
        packet_out[k, :kv_rows, :] = kv_in[k][:, SPAN:]
        packet_out[k, kv_rows:, :] = digits.astype(jnp.float32).astype(jnp.bfloat16)
    back(packet_out, packet)
    for copy in copies[2:4]:
        copy.wait()
    back(ffn_out, ffn_half)
    for copy in copies[4:]:
        copy.wait()
    back(attention_out, attention_half)
    for copy in backs:
        copy.wait()


def gather_kernel(blocks, here, host, index, before, gain, *refs):
    *db_refs, rows_out, normed_out = refs
    per_host, part_rows, width = db_refs[0].shape
    seq = here[0]
    for i in range(CH_DEV * NEIGH):
        span, k = i // NEIGH, i % NEIGH
        if span == 0:
            of_host, place = before[k, 0] // per_host, before[k, 0] % per_host
        else:
            of_host, place = host[k, span - 1], index[k, span - 1]
        block = (seq // 2 - of_host // 2 + blocks) % blocks * 2 + (seq + of_host) % 2
        for b in range(2 * blocks):

            @pl.when(block == b)
            def _(b=b, place=place, i=i):
                rows_out[i * part_rows : (i + 1) * part_rows, :] = db_refs[b][place]

    for at in range(0, rows_out.shape[0], NORM_BLOCK):
        values = rows_out[at : at + NORM_BLOCK, :].astype(jnp.float32)
        normed_out[at : at + NORM_BLOCK, :] = rms_scale(values, gain[...]).astype(jnp.bfloat16)


def attention_kernel(pieces, far, seq_index, before, normed_in, *refs):
    weight_refs, kv_refs, (result,) = refs[: 2 * pieces], refs[2 * pieces : 3 * pieces], refs[3 * pieces :]
    rows, width = before.shape
    span_rows = rows // CH_DEV
    pair_rows = 2 * span_rows
    pad = HEAD_DIM - EHEAD_DIM
    scale = float(EHEAD_DIM) ** (-0.5)
    odd = seq_index[0] % 2
    lane = lax.broadcasted_iota(jnp.int32, (pair_rows, 2 * SPAN), 1)
    row = lax.broadcasted_iota(jnp.int32, (pair_rows, 2 * SPAN), 0)
    own_lanes = (lane < SPAN) == (row < span_rows)
    rest = jnp.zeros((pad, 2 * SPAN), jnp.bfloat16)
    empty = jnp.zeros((HEAD_DIM, 2 * SPAN), jnp.bfloat16)
    ones = jnp.ones((2 * HEAD_DIM - EHEAD_DIM, 2 * SPAN), jnp.bfloat16)
    weight_rest = jnp.zeros((pad, width), jnp.bfloat16)
    q_parts, out_parts = [], []
    for p in range(pieces):
        first, second = weight_refs[2 * p][...], weight_refs[2 * p + 1][...]
        if far:
            first, second = (
                jnp.where(odd == 0, first, second),
                jnp.where(odd == 0, second, first),
            )
            q_parts += [first[:EHEAD_DIM], weight_rest, second[:EHEAD_DIM], weight_rest]
            out_parts += [first[EHEAD_DIM:], weight_rest, second[EHEAD_DIM:], weight_rest]
        else:
            q_parts += [first[:EHEAD_DIM], weight_rest, first[EHEAD_DIM:], weight_rest]
            out_parts += [second[:EHEAD_DIM], weight_rest, second[EHEAD_DIM:], weight_rest]
    q_w, out_w = jnp.concatenate(q_parts, axis=0), jnp.concatenate(out_parts, axis=0)
    left = lax.broadcasted_iota(jnp.int32, (BLOCK, 2 * SPAN), 1) < SPAN
    for start in range(0, rows, BLOCK):
        block = slice(start, start + BLOCK)
        query = (mxu(normed_in[block, :], q_w, NT) * scale).astype(jnp.bfloat16)
        attended = []
        for p in range(pieces):
            scores = []
            for at in range(0, BLOCK, pair_rows):
                tok = (start + at) // pair_rows * 2 * SPAN
                keys = kv_refs[p][0, :, tok : tok + 2 * SPAN]
                keys = jnp.concatenate(
                    [
                        jnp.concatenate([keys[:EHEAD_DIM], rest, empty], axis=0),
                        jnp.concatenate([empty, turned(keys[EHEAD_DIM:]), rest], axis=0),
                    ],
                    axis=1,
                )
                of_piece = query[at : at + pair_rows, 2 * HEAD_DIM * p : 2 * HEAD_DIM * (p + 1)]
                both = mxu(of_piece, keys, NN)
                scores.append(jnp.where(own_lanes, both[:, : 2 * SPAN], both[:, 2 * SPAN :]))
            scores = jnp.concatenate(scores, axis=0)
            low = jnp.max(jnp.where(left, scores, -jnp.inf), axis=1, keepdims=True)
            high = jnp.max(jnp.where(left, -jnp.inf, scores), axis=1, keepdims=True)
            weights = jnp.exp(scores - jnp.where(left, low, high)).astype(jnp.bfloat16)
            of_heads = [[], []]
            for at in range(0, BLOCK, pair_rows):
                tok = (start + at) // pair_rows * 2 * SPAN
                part = weights[at : at + pair_rows]
                vals = kv_refs[p][1, :, tok : tok + 2 * SPAN]
                for head in range(2):
                    picked = jnp.where(own_lanes if head == 0 else ~own_lanes, part, jnp.zeros_like(part))
                    of_head = vals[:EHEAD_DIM] if head == 0 else turned(vals[EHEAD_DIM:])
                    mixed = mxu(picked, jnp.concatenate([of_head, ones], axis=0), NT)
                    of_heads[head].append((mixed[:, :HEAD_DIM] / mixed[:, HEAD_DIM:]).astype(jnp.bfloat16))
            attended += [jnp.concatenate(parts, axis=0) for parts in of_heads]
        added = mxu(jnp.concatenate(attended, axis=1), out_w, NN)
        result[block, :] = before[block, :].astype(jnp.float32) + added


def ffn_kernel(far, first, gain, before, *refs):
    if first:
        *group_refs, result, normed = refs
    else:
        normed, *group_refs, result = refs
    if far:
        half = group_refs[0].shape[0] // 2
        ups, downs = [r[:half] for r in group_refs], [r[half:] for r in group_refs]
    else:
        ups, downs = [r[...] for r in group_refs[::2]], [r[...] for r in group_refs[1::2]]
    up, down = jnp.concatenate(ups, axis=0), jnp.concatenate(downs, axis=0)
    raised = []
    for start in range(0, before.shape[0], BLOCK):
        block = slice(start, start + BLOCK)
        if first:
            for at in range(start, start + BLOCK, NORM_BLOCK):
                values = rms_scale(before[at : at + NORM_BLOCK, :], gain[...])
                normed[at : at + NORM_BLOCK, :] = values.astype(jnp.bfloat16)
        raised.append(mxu(normed[block, :], up, NT).astype(jnp.bfloat16))
    for i, units in enumerate(raised):
        block = slice(i * BLOCK, (i + 1) * BLOCK)
        added = before[block, :] + mxu(jax.nn.gelu(units), down, NN)
        result[block, :] = added.astype(result.dtype)


def pairs_kernel(encoded, weights, pairs):
    pairs[...] = mxu(encoded[...], weights[...], NN).astype(jnp.bfloat16)


def decoder_kernel(first, own_pairs, other, weights, queries, out, other_pairs, held, sems):
    rows = other.shape[0]
    part = rows // CH_DEV
    width = queries.shape[1]
    scale = float(HEAD_DIM) ** (-0.5)
    other_pairs[...] = mxu(other[...], weights[...], NN).astype(jnp.bfloat16)

    def span_pairs_of(span, col):
        return jnp.concatenate(
            [r[span * part : (span + 1) * part, col : col + HEAD_DIM] for r in (own_pairs, other_pairs)],
            axis=0,
        )

    ones = jnp.ones((2 * part, HEAD_DIM), jnp.bfloat16)
    copies = []
    for head in range(width // HEAD_DIM):
        col = head * HEAD_DIM
        query = (queries[:, col : col + HEAD_DIM].astype(jnp.float32) * scale).astype(jnp.bfloat16)
        scores = jnp.concatenate(
            [
                mxu(query[span * SPAN : (span + 1) * SPAN], span_pairs_of(span, col), NT)
                for span in range(CH_DEV)
            ],
            axis=0,
        )
        weights_b = jnp.exp(scores - jnp.max(scores, axis=1, keepdims=True)).astype(jnp.bfloat16)
        for span in range(CH_DEV):
            vals = jnp.concatenate([span_pairs_of(span, width + col), ones], axis=1)
            result = mxu(weights_b[span * SPAN : (span + 1) * SPAN], vals, NN)
            result = result[:, :HEAD_DIM] / result[:, HEAD_DIM:]
            if span == 0:
                result = jnp.where(first[0] == 0, jnp.zeros_like(result), result)
            held[head, span * SPAN : (span + 1) * SPAN, :] = result
        copies.append(
            pltpu.make_async_copy(held.at[head], out.at[:, pl.ds(col, HEAD_DIM)], sems.at[head])
        )
        copies[-1].start()
    for copy in copies:
        copy.wait()


def call(body, out_shape, in_specs, name, flops, vmem_mib, scratch=(), out="v"):
    spaces = {"s": pltpu.SMEM, "v": pltpu.VMEM, "h": pl.ANY}
    return pl.pallas_call(
        body,
        out_shape=out_shape,
        in_specs=[pl.BlockSpec(memory_space=spaces[c]) for c in in_specs],
        out_specs=jax.tree.map(lambda _: pl.BlockSpec(memory_space=spaces[out]), out_shape),
        scratch_shapes=list(scratch),
        compiler_params=pltpu.CompilerParams(vmem_limit_bytes=vmem_mib * 1024 * 1024),
        cost_estimate=pl.CostEstimate(flops=flops, bytes_accessed=8_000_000, transcendentals=0),
        name=name,
    )


def on_device(
    span_pairs,
    dec_queries,
    database,
    nbr_index,
    nbr_host,
    enc_gain,
    enc_query,
    enc_out,
    ffn_gain,
    ffn_up,
    ffn_down,
    dec_kv,
):
    seq_size = lax.axis_size("seq")
    lanes = lax.axis_size("mp")
    seq_index = lax.axis_index("seq")
    lane_index = lax.axis_index("mp")
    entries_here, block_rows, width = database.shape
    half_rows = block_rows // HALVES
    rows = CH_DEV * NEIGH * half_rows
    blocks = seq_size // 2

    def core_swap(array):
        return lax.ppermute(array, "mp", [(i, i ^ 1) for i in range(lanes)])

    def lane_step(array, step):
        return lax.ppermute(array, "mp", [(i, (i + 2 * step) % lanes) for i in range(lanes)])

    def seq_swap(array):
        return lax.ppermute(array, "seq", [(i, i ^ 1) for i in range(seq_size)])

    def seq_cross(array):
        return lax.ppermute(array, "seq", [(i, i ^ 2) for i in range(seq_size)])

    def seq_ring(array, way):
        return lax.ppermute(array, "seq", [(i, (i + 2 * way) % seq_size) for i in range(seq_size)])

    def next_seq(array):
        return lax.ppermute(array, "seq", [(i, i + 1) for i in range(seq_size - 1)])

    query_t, up_t = enc_query.T, ffn_up.T
    kv_t = jnp.transpose(span_pairs, (1, 2, 0))
    kv_rows, tokens = kv_t.shape[1:]
    kept = tokens - SPAN

    here = seq_index.reshape(1).astype(jnp.int32)
    lane_here = lane_index.reshape(1).astype(jnp.int32)
    host, index = nbr_host.T, nbr_index.T
    dma = pltpu.SemaphoreType.DMA
    short = functools.partial(jax.ShapeDtypeStruct, dtype=jnp.bfloat16)
    database_half, attention_half, ffn_half, packet = call(
        prepare_kernel,
        (
            short((entries_here, half_rows, width)),
            short(enc_out.shape),
            short(ffn_down.shape),
            short((2, kv_rows + 16, SPAN)),
        ),
        "ssss" + "h" * 6,
        "prepare",
        rows * width,
        60,
        scratch=[
            pltpu.VMEM((entries_here, half_rows, width), jnp.float32),
            pltpu.VMEM((entries_here, half_rows, width), jnp.bfloat16),
            pltpu.VMEM((2, kv_rows, 2 * SPAN), jnp.bfloat16),
            pltpu.VMEM((2, kv_rows + 16, SPAN), jnp.bfloat16),
            pltpu.VMEM(enc_out.shape, jnp.bfloat16),
            pltpu.VMEM(ffn_down.shape, jnp.bfloat16),
            dma((10,)),
        ],
        out="h",
    )(here, lane_here, host, index, database, query_t, enc_out, up_t, ffn_down, kv_t)

    dec_width = dec_kv.shape[2]
    middle, last = blocks // 2, blocks - 1
    names = {"0": 0, "n": 1, "p": last, "m": middle}
    short_name = {place: name for name, place in names.items()}
    arrived = {}

    def got(name):
        if name not in arrived:
            arrived[name] = makers[name]()
        return arrived[name]

    def ready(name, array):
        others = [got(other) for other in ORDER.get(name, ())]
        return lax.optimization_barrier((array, others))[0] if others else array

    def database(place):
        if place == 0:
            return database_half
        way = 1 if place <= middle else -1
        source = database_at((place - way) % blocks)
        return seq_ring(ready(f"z{short_name.get(place, place)}", source), way)

    def database_at(place):
        return got(f"z{short_name.get(place, place)}")

    def swapped_at(place):
        return got(f"x{short_name.get(place, place)}")

    def received_keys():
        return jnp.concatenate([got("pk")[:, :kv_rows], kv_t[:, :, :kept]], axis=2)

    def both_cores(name, arrays):
        return tuple(core_swap(a) for a in ready(name, arrays))

    makers = {
        "ya": lambda: lane_step(ready("ya", attention_half), 1),
        "yf": lambda: lane_step(ready("yf", ffn_half), 1),
        "yk": lambda: lane_step(ready("yk", got("keys")), 1),
        "pk": lambda: next_seq(ready("pk", packet)),
        "keys": lambda: ready("keys", received_keys()),
        "xa": lambda: seq_swap(ready("xa", got("ya"))),
        "zf": lambda: seq_cross(ready("zf", got("yf"))),
        "ca": lambda: both_cores("ca", (query_t, enc_out)),
        "cf": lambda: both_cores("cf", (up_t, ffn_down)),
        "ck": lambda: core_swap(ready("ck", got("keys"))),
        "cya": lambda: core_swap(ready("cya", got("ya"))),
        "cyk": lambda: core_swap(ready("cyk", got("yk"))),
        "cyf": lambda: core_swap(ready("cyf", got("yf"))),
        "cxa": lambda: core_swap(ready("cxa", got("xa"))),
        "czf": lambda: core_swap(ready("czf", got("zf"))),
        "wk": lambda: ready("wk", dec_kv.reshape(width, 2 * dec_width)),
    }
    for place in range(blocks):
        name = short_name.get(place, place)
        makers[f"z{name}"] = functools.partial(database, place)
        makers[f"x{name}"] = lambda place=place, name=name: seq_swap(ready(f"x{name}", database_at(place)))
    enc_gain, ffn_gain = enc_gain.reshape(1, width), ffn_gain.reshape(1, width)
    enc_gain, ffn_gain = ready("gains", (enc_gain, ffn_gain))

    gemm = 2 * rows * width * width
    long_rows = jax.ShapeDtypeStruct((rows, width), jnp.float32)
    short_rows = short((rows, width))
    before = got("pk")[:, kv_rows : kv_rows + 2, 0].astype(jnp.int32)
    before = before[:, :1] * DIGIT + before[:, 1:]
    database_blocks = [a for place in range(blocks) for a in (database_at(place), swapped_at(place))]
    values, normed = call(
        functools.partial(gather_kernel, blocks),
        (short_rows, short_rows),
        "ssss" + "v" * (1 + 2 * blocks),
        "neighbour_rows",
        10 * rows * width,
        16 + (8 * blocks * database_half.size >> 20),
    )(ready("gather", here), host, index, before, enc_gain, *database_blocks)

    def attention(so_far, weights, kv, far):
        return call(
            functools.partial(attention_kernel, len(kv), far),
            long_rows,
            "svv" + "v" * 3 * len(kv),
            "encoder_attention",
            gemm * 2 * len(kv) // lanes,
            24,
        )(here, so_far, normed, *weights, *kv)

    arrived["near"] = attention(
        ready("near", values), (query_t, enc_out, *got("ca")), (got("keys"), got("ck")), False
    )
    far_weights = (got("ya"), got("xa"), got("cya"), got("cxa"))
    resid = attention(got("near"), far_weights, (got("yk"), got("cyk")), True)
    arrived["far"] = resid

    near_units = (up_t, ffn_down, *got("cf"))
    partial_rows, normed = call(
        functools.partial(ffn_kernel, False, True),
        (long_rows, short_rows),
        "vv" + "v" * len(near_units),
        "encoder_ffn_near",
        2 * gemm,
        30,
    )(ffn_gain, resid, *near_units)
    arrived["units"] = partial_rows
    far_units = [got(name) for name in ("yf", "cyf", "zf", "czf")]
    encoded = call(
        functools.partial(ffn_kernel, True, False),
        short_rows,
        "vvv" + "v" * len(far_units),
        "encoder_ffn_far",
        2 * gemm,
        30,
    )(ffn_gain, partial_rows, normed, *far_units)

    other = core_swap(encoded)
    pairs_shape = (rows, 2 * dec_width)
    pairs_flops = 2 * rows * width * 2 * dec_width
    own_pairs = call(
        pairs_kernel,
        jax.ShapeDtypeStruct(pairs_shape, jnp.bfloat16),
        "vv",
        "decoder_pairs",
        pairs_flops,
        20,
    )(encoded, got("wk"))
    return call(
        decoder_kernel,
        jax.ShapeDtypeStruct(dec_queries.shape, jnp.float32),
        "svvvv",
        "decoder_attention",
        pairs_flops,
        28,
        scratch=[
            pltpu.VMEM(pairs_shape, jnp.bfloat16),
            pltpu.VMEM((dec_width // HEAD_DIM, dec_queries.shape[0], HEAD_DIM), jnp.float32),
            dma((dec_width // HEAD_DIM,)),
        ],
        out="h",
    )(here, own_pairs, other, got("wk"), dec_queries)


def solution(mesh):
    placed = (
        P("seq", None, "mp"),
        P("seq", "mp"),
        P("seq", None, None),
        P("seq", None),
        P("seq", None),
        P(),
        P(None, "mp"),
        P("mp", None),
        P(),
        P(None, "mp"),
        P("mp", None),
        P(None, None, "mp"),
    )
    return jax.shard_map(
        on_device, mesh=mesh, in_specs=placed, out_specs=P("seq", "mp"), check_vma=False
    )
```

```python
import functools

import jax
import jax.numpy as jnp
from jax import lax
from jax.experimental import pallas as pl
from jax.experimental.pallas import tpu as pltpu
from jax.sharding import PartitionSpec as P

HEAD_DIM = 128
EHEAD_DIM = 112
SPAN = 64
NBL = 128
NEIGH = 2
CH_DEV = 8
HALVES = 2
BLOCK = 512
NORM_BLOCK = 64
DIGIT = 128

ORDER = {
    "pk": ("x0",),
    "xp": ("xn",),
    "xa": ("xm", "ca"),
    "zm": ("x0",),
    "ca": ("xn",),
    "cf": ("xn",),
    "keys": ("xp",),
    "yk": ("yf", "xm",),
    "cya": ("yf",),
    "cyf": ("far",),
    "cyk": ("near",),
    "czf": ("far",),
    "near": ("yf",),
    "wk": ("ya",),
    "gains": ("zn",),
}

NT = (((1,), (1,)), ((), ()))
NN = (((1,), (0,)), ((), ()))


def mxu(lhs, rhs, dims):
    return lax.dot_general(lhs, rhs, dims, preferred_element_type=jnp.float32)


def rms_scale(values, gain):
    return values * lax.rsqrt(jnp.mean(values * values, axis=-1, keepdims=True) + 1e-06) * gain


def turned(chunk):
    return jnp.concatenate([chunk[:, SPAN:], chunk[:, :SPAN]], axis=1)


def prepare_kernel(here, lane_here, host, index, database, query_t, enc_out, up_t, down, kv_t, *refs):
    db_half, attention_half, ffn_half, packet = refs[:4]
    db_in, db_out, kv_in, packet_out, attention_out, ffn_out, sems = refs[4:]
    per_host, half_rows, width = db_half.shape
    seq, lane = here[0], lane_here[0]
    copies = [
        pltpu.make_async_copy(
            database.at[:, pl.ds(pl.multiple_of(lane % HALVES * half_rows, half_rows), half_rows)],
            db_in,
            sems.at[0],
        ),
        pltpu.make_async_copy(kv_t.at[:, :, pl.ds(kv_t.shape[2] - 2 * SPAN, 2 * SPAN)], kv_in, sems.at[1]),
    ]
    halves = ((up_t, ffn_out, 0, seq // 2 % 2), (down, ffn_out, 1, seq // 2 % 2))
    halves += ((query_t, attention_out, 0, seq % 2), (enc_out, attention_out, 1, seq % 2))
    for i, (source, target, spot, parity) in enumerate(halves):
        count = source.shape[0] // 2
        copies.append(
            pltpu.make_async_copy(
                source.at[pl.ds(pl.multiple_of(parity * count, 16), count)],
                target.at[pl.ds(spot * count, count)],
                sems.at[2 + i],
            )
        )
    for copy in copies:
        copy.start()
    backs = []

    def back(source, target):
        backs.append(pltpu.make_async_copy(source, target, sems.at[6 + len(backs)]))
        backs[-1].start()

    copies[0].wait()
    db_out[...] = db_in[...].astype(jnp.bfloat16)
    back(db_out, db_half)
    copies[1].wait()
    kv_rows = kv_in.shape[1]
    row = lax.broadcasted_iota(jnp.int32, (packet.shape[1] - kv_rows, SPAN), 0)
    for k in range(NEIGH):
        entry = host[k, CH_DEV - 1] * per_host + index[k, CH_DEV - 1]
        digits = jnp.where(row == 0, entry // DIGIT, jnp.where(row == 1, entry % DIGIT, 0))
        packet_out[k, :kv_rows, :] = kv_in[k][:, SPAN:]
        packet_out[k, kv_rows:, :] = digits.astype(jnp.float32).astype(jnp.bfloat16)
    back(packet_out, packet)
    for copy in copies[2:4]:
        copy.wait()
    back(ffn_out, ffn_half)
    for copy in copies[4:]:
        copy.wait()
    back(attention_out, attention_half)
    for copy in backs:
        copy.wait()


def gather_kernel(blocks, here, host, index, before, gain, *refs):
    *db_refs, rows_out, normed_out = refs
    per_host, part_rows, width = db_refs[0].shape
    seq = here[0]
    for i in range(CH_DEV * NEIGH):
        span, k = i // NEIGH, i % NEIGH
        if span == 0:
            of_host, place = before[k, 0] // per_host, before[k, 0] % per_host
        else:
            of_host, place = host[k, span - 1], index[k, span - 1]
        block = (seq // 2 - of_host // 2 + blocks) % blocks * 2 + (seq + of_host) % 2
        for b in range(2 * blocks):

            @pl.when(block == b)
            def _(b=b, place=place, i=i):
                rows_out[i * part_rows : (i + 1) * part_rows, :] = db_refs[b][place]

    for at in range(0, rows_out.shape[0], NORM_BLOCK):
        values = rows_out[at : at + NORM_BLOCK, :].astype(jnp.float32)
        normed_out[at : at + NORM_BLOCK, :] = rms_scale(values, gain[...]).astype(jnp.bfloat16)


def attention_kernel(pieces, far, seq_index, before, normed_in, *refs):
    weight_refs, kv_refs, (result,) = refs[: 2 * pieces], refs[2 * pieces : 3 * pieces], refs[3 * pieces :]
    rows, width = before.shape
    span_rows = rows // CH_DEV
    pair_rows = 2 * span_rows
    pad = HEAD_DIM - EHEAD_DIM
    scale = float(EHEAD_DIM) ** (-0.5)
    odd = seq_index[0] % 2
    lane = lax.broadcasted_iota(jnp.int32, (pair_rows, 2 * SPAN), 1)
    row = lax.broadcasted_iota(jnp.int32, (pair_rows, 2 * SPAN), 0)
    own_lanes = (lane < SPAN) == (row < span_rows)
    rest = jnp.zeros((pad, 2 * SPAN), jnp.bfloat16)
    empty = jnp.zeros((HEAD_DIM, 2 * SPAN), jnp.bfloat16)
    ones = jnp.ones((2 * HEAD_DIM - EHEAD_DIM, 2 * SPAN), jnp.bfloat16)
    weight_rest = jnp.zeros((pad, width), jnp.bfloat16)
    q_parts, out_parts = [], []
    for p in range(pieces):
        first, second = weight_refs[2 * p][...], weight_refs[2 * p + 1][...]
        if far:
            first, second = (
                jnp.where(odd == 0, first, second),
                jnp.where(odd == 0, second, first),
            )
            q_parts += [first[:EHEAD_DIM], weight_rest, second[:EHEAD_DIM], weight_rest]
            out_parts += [first[EHEAD_DIM:], weight_rest, second[EHEAD_DIM:], weight_rest]
        else:
            q_parts += [first[:EHEAD_DIM], weight_rest, first[EHEAD_DIM:], weight_rest]
            out_parts += [second[:EHEAD_DIM], weight_rest, second[EHEAD_DIM:], weight_rest]
    q_w, out_w = jnp.concatenate(q_parts, axis=0), jnp.concatenate(out_parts, axis=0)
    left = lax.broadcasted_iota(jnp.int32, (BLOCK, 2 * SPAN), 1) < SPAN
    for start in range(0, rows, BLOCK):
        block = slice(start, start + BLOCK)
        query = (mxu(normed_in[block, :], q_w, NT) * scale).astype(jnp.bfloat16)
        attended = []
        for p in range(pieces):
            scores = []
            for at in range(0, BLOCK, pair_rows):
                tok = (start + at) // pair_rows * 2 * SPAN
                keys = kv_refs[p][0, :, tok : tok + 2 * SPAN]
                keys = jnp.concatenate(
                    [
                        jnp.concatenate([keys[:EHEAD_DIM], rest, empty], axis=0),
                        jnp.concatenate([empty, turned(keys[EHEAD_DIM:]), rest], axis=0),
                    ],
                    axis=1,
                )
                of_piece = query[at : at + pair_rows, 2 * HEAD_DIM * p : 2 * HEAD_DIM * (p + 1)]
                both = mxu(of_piece, keys, NN)
                scores.append(jnp.where(own_lanes, both[:, : 2 * SPAN], both[:, 2 * SPAN :]))
            scores = jnp.concatenate(scores, axis=0)
            low = jnp.max(jnp.where(left, scores, -jnp.inf), axis=1, keepdims=True)
            high = jnp.max(jnp.where(left, -jnp.inf, scores), axis=1, keepdims=True)
            weights = jnp.exp(scores - jnp.where(left, low, high)).astype(jnp.bfloat16)
            of_heads = [[], []]
            for at in range(0, BLOCK, pair_rows):
                tok = (start + at) // pair_rows * 2 * SPAN
                part = weights[at : at + pair_rows]
                vals = kv_refs[p][1, :, tok : tok + 2 * SPAN]
                for head in range(2):
                    picked = jnp.where(own_lanes if head == 0 else ~own_lanes, part, jnp.zeros_like(part))
                    of_head = vals[:EHEAD_DIM] if head == 0 else turned(vals[EHEAD_DIM:])
                    mixed = mxu(picked, jnp.concatenate([of_head, ones], axis=0), NT)
                    of_heads[head].append((mixed[:, :HEAD_DIM] / mixed[:, HEAD_DIM:]).astype(jnp.bfloat16))
            attended += [jnp.concatenate(parts, axis=0) for parts in of_heads]
        added = mxu(jnp.concatenate(attended, axis=1), out_w, NN)
        result[block, :] = before[block, :].astype(jnp.float32) + added


def ffn_kernel(far, first, gain, before, *refs):
    if first:
        *group_refs, result, normed = refs
    else:
        normed, *group_refs, result = refs
    if far:
        half = group_refs[0].shape[0] // 2
        ups, downs = [r[:half] for r in group_refs], [r[half:] for r in group_refs]
    else:
        ups, downs = [r[...] for r in group_refs[::2]], [r[...] for r in group_refs[1::2]]
    up, down = jnp.concatenate(ups, axis=0), jnp.concatenate(downs, axis=0)
    raised = []
    for start in range(0, before.shape[0], BLOCK):
        block = slice(start, start + BLOCK)
        if first:
            for at in range(start, start + BLOCK, NORM_BLOCK):
                values = rms_scale(before[at : at + NORM_BLOCK, :], gain[...])
                normed[at : at + NORM_BLOCK, :] = values.astype(jnp.bfloat16)
        raised.append(mxu(normed[block, :], up, NT).astype(jnp.bfloat16))
    for i, units in enumerate(raised):
        block = slice(i * BLOCK, (i + 1) * BLOCK)
        added = before[block, :] + mxu(jax.nn.gelu(units), down, NN)
        result[block, :] = added.astype(result.dtype)


def pairs_kernel(encoded, weights, pairs):
    pairs[...] = mxu(encoded[...], weights[...], NN).astype(jnp.bfloat16)


def decoder_kernel(first, own_pairs, other, weights, queries, out, other_pairs, held, sems):
    rows = other.shape[0]
    part = rows // CH_DEV
    width = queries.shape[1]
    scale = float(HEAD_DIM) ** (-0.5)
    other_pairs[...] = mxu(other[...], weights[...], NN).astype(jnp.bfloat16)

    def span_pairs_of(span, col):
        return jnp.concatenate(
            [r[span * part : (span + 1) * part, col : col + HEAD_DIM] for r in (own_pairs, other_pairs)],
            axis=0,
        )

    ones = jnp.ones((2 * part, HEAD_DIM), jnp.bfloat16)
    copies = []
    for head in range(width // HEAD_DIM):
        col = head * HEAD_DIM
        query = (queries[:, col : col + HEAD_DIM].astype(jnp.float32) * scale).astype(jnp.bfloat16)
        scores = jnp.concatenate(
            [
                mxu(query[span * SPAN : (span + 1) * SPAN], span_pairs_of(span, col), NT)
                for span in range(CH_DEV)
            ],
            axis=0,
        )
        weights_b = jnp.exp(scores - jnp.max(scores, axis=1, keepdims=True)).astype(jnp.bfloat16)
        for span in range(CH_DEV):
            vals = jnp.concatenate([span_pairs_of(span, width + col), ones], axis=1)
            result = mxu(weights_b[span * SPAN : (span + 1) * SPAN], vals, NN)
            result = result[:, :HEAD_DIM] / result[:, HEAD_DIM:]
            if span == 0:
                result = jnp.where(first[0] == 0, jnp.zeros_like(result), result)
            held[head, span * SPAN : (span + 1) * SPAN, :] = result
        copies.append(
            pltpu.make_async_copy(held.at[head], out.at[:, pl.ds(col, HEAD_DIM)], sems.at[head])
        )
        copies[-1].start()
    for copy in copies:
        copy.wait()


def call(body, out_shape, in_specs, name, flops, vmem_mib, scratch=(), out="v"):
    spaces = {"s": pltpu.SMEM, "v": pltpu.VMEM, "h": pl.ANY}
    return pl.pallas_call(
        body,
        out_shape=out_shape,
        in_specs=[pl.BlockSpec(memory_space=spaces[c]) for c in in_specs],
        out_specs=jax.tree.map(lambda _: pl.BlockSpec(memory_space=spaces[out]), out_shape),
        scratch_shapes=list(scratch),
        compiler_params=pltpu.CompilerParams(vmem_limit_bytes=vmem_mib * 1024 * 1024),
        cost_estimate=pl.CostEstimate(flops=flops, bytes_accessed=8_000_000, transcendentals=0),
        name=name,
    )


def on_device(
    span_pairs,
    dec_queries,
    database,
    nbr_index,
    nbr_host,
    enc_gain,
    enc_query,
    enc_out,
    ffn_gain,
    ffn_up,
    ffn_down,
    dec_kv,
):
    seq_size = lax.axis_size("seq")
    lanes = lax.axis_size("mp")
    seq_index = lax.axis_index("seq")
    lane_index = lax.axis_index("mp")
    entries_here, block_rows, width = database.shape
    half_rows = block_rows // HALVES
    rows = CH_DEV * NEIGH * half_rows
    blocks = seq_size // 2

    def core_swap(array):
        return lax.ppermute(array, "mp", [(i, i ^ 1) for i in range(lanes)])

    def lane_step(array, step):
        return lax.ppermute(array, "mp", [(i, (i + 2 * step) % lanes) for i in range(lanes)])

    def seq_swap(array):
        return lax.ppermute(array, "seq", [(i, i ^ 1) for i in range(seq_size)])

    def seq_cross(array):
        return lax.ppermute(array, "seq", [(i, i ^ 2) for i in range(seq_size)])

    def seq_ring(array, way):
        return lax.ppermute(array, "seq", [(i, (i + 2 * way) % seq_size) for i in range(seq_size)])

    def next_seq(array):
        return lax.ppermute(array, "seq", [(i, i + 1) for i in range(seq_size - 1)])

    query_t, up_t = enc_query.T, ffn_up.T
    kv_t = jnp.transpose(span_pairs, (1, 2, 0))
    kv_rows, tokens = kv_t.shape[1:]
    kept = tokens - SPAN

    here = seq_index.reshape(1).astype(jnp.int32)
    lane_here = lane_index.reshape(1).astype(jnp.int32)
    host, index = nbr_host.T, nbr_index.T
    dma = pltpu.SemaphoreType.DMA
    short = functools.partial(jax.ShapeDtypeStruct, dtype=jnp.bfloat16)
    database_half, attention_half, ffn_half, packet = call(
        prepare_kernel,
        (
            short((entries_here, half_rows, width)),
            short(enc_out.shape),
            short(ffn_down.shape),
            short((2, kv_rows + 16, SPAN)),
        ),
        "ssss" + "h" * 6,
        "prepare",
        rows * width,
        60,
        scratch=[
            pltpu.VMEM((entries_here, half_rows, width), jnp.float32),
            pltpu.VMEM((entries_here, half_rows, width), jnp.bfloat16),
            pltpu.VMEM((2, kv_rows, 2 * SPAN), jnp.bfloat16),
            pltpu.VMEM((2, kv_rows + 16, SPAN), jnp.bfloat16),
            pltpu.VMEM(enc_out.shape, jnp.bfloat16),
            pltpu.VMEM(ffn_down.shape, jnp.bfloat16),
            dma((10,)),
        ],
        out="h",
    )(here, lane_here, host, index, database, query_t, enc_out, up_t, ffn_down, kv_t)

    dec_width = dec_kv.shape[2]
    middle, last = blocks // 2, blocks - 1
    names = {"0": 0, "n": 1, "p": last, "m": middle}
    short_name = {place: name for name, place in names.items()}
    arrived = {}

    def got(name):
        if name not in arrived:
            arrived[name] = makers[name]()
        return arrived[name]

    def ready(name, array):
        others = [got(other) for other in ORDER.get(name, ())]
        return lax.optimization_barrier((array, others))[0] if others else array

    def database(place):
        if place == 0:
            return database_half
        way = 1 if place <= middle else -1
        source = database_at((place - way) % blocks)
        return seq_ring(ready(f"z{short_name.get(place, place)}", source), way)

    def database_at(place):
        return got(f"z{short_name.get(place, place)}")

    def swapped_at(place):
        return got(f"x{short_name.get(place, place)}")

    def received_keys():
        return jnp.concatenate([got("pk")[:, :kv_rows], kv_t[:, :, :kept]], axis=2)

    def both_cores(name, arrays):
        return tuple(core_swap(a) for a in ready(name, arrays))

    makers = {
        "ya": lambda: lane_step(ready("ya", attention_half), 1),
        "yf": lambda: lane_step(ready("yf", ffn_half), 1),
        "yk": lambda: lane_step(ready("yk", got("keys")), 1),
        "pk": lambda: next_seq(ready("pk", packet)),
        "keys": lambda: ready("keys", received_keys()),
        "xa": lambda: seq_swap(ready("xa", got("ya"))),
        "zf": lambda: seq_cross(ready("zf", got("yf"))),
        "ca": lambda: both_cores("ca", (query_t, enc_out)),
        "cf": lambda: both_cores("cf", (up_t, ffn_down)),
        "ck": lambda: core_swap(ready("ck", got("keys"))),
        "cya": lambda: core_swap(ready("cya", got("ya"))),
        "cyk": lambda: core_swap(ready("cyk", got("yk"))),
        "cyf": lambda: core_swap(ready("cyf", got("yf"))),
        "cxa": lambda: core_swap(ready("cxa", got("xa"))),
        "czf": lambda: core_swap(ready("czf", got("zf"))),
        "wk": lambda: ready("wk", dec_kv.reshape(width, 2 * dec_width)),
    }
    for place in range(blocks):
        name = short_name.get(place, place)
        makers[f"z{name}"] = functools.partial(database, place)
        makers[f"x{name}"] = lambda place=place, name=name: seq_swap(ready(f"x{name}", database_at(place)))
    enc_gain, ffn_gain = enc_gain.reshape(1, width), ffn_gain.reshape(1, width)
    enc_gain, ffn_gain = ready("gains", (enc_gain, ffn_gain))

    gemm = 2 * rows * width * width
    long_rows = jax.ShapeDtypeStruct((rows, width), jnp.float32)
    short_rows = short((rows, width))
    before = got("pk")[:, kv_rows : kv_rows + 2, 0].astype(jnp.int32)
    before = before[:, :1] * DIGIT + before[:, 1:]
    database_blocks = [a for place in range(blocks) for a in (database_at(place), swapped_at(place))]
    values, normed = call(
        functools.partial(gather_kernel, blocks),
        (short_rows, short_rows),
        "ssss" + "v" * (1 + 2 * blocks),
        "neighbour_rows",
        10 * rows * width,
        16 + (8 * blocks * database_half.size >> 20),
    )(ready("gather", here), host, index, before, enc_gain, *database_blocks)

    def attention(so_far, weights, kv, far):
        return call(
            functools.partial(attention_kernel, len(kv), far),
            long_rows,
            "svv" + "v" * 3 * len(kv),
            "encoder_attention",
            gemm * 2 * len(kv) // lanes,
            24,
        )(here, so_far, normed, *weights, *kv)

    arrived["near"] = attention(
        ready("near", values), (query_t, enc_out, *got("ca")), (got("keys"), got("ck")), False
    )
    far_weights = (got("ya"), got("xa"), got("cya"), got("cxa"))
    resid = attention(got("near"), far_weights, (got("yk"), got("cyk")), True)
    arrived["far"] = resid

    near_units = (up_t, ffn_down, *got("cf"))
    partial_rows, normed = call(
        functools.partial(ffn_kernel, False, True),
        (long_rows, short_rows),
        "vv" + "v" * len(near_units),
        "encoder_ffn_near",
        2 * gemm,
        30,
    )(ffn_gain, resid, *near_units)
    arrived["units"] = partial_rows
    far_units = [got(name) for name in ("yf", "cyf", "zf", "czf")]
    encoded = call(
        functools.partial(ffn_kernel, True, False),
        short_rows,
        "vvv" + "v" * len(far_units),
        "encoder_ffn_far",
        2 * gemm,
        30,
    )(ffn_gain, partial_rows, normed, *far_units)

    other = core_swap(encoded)
    pairs_shape = (rows, 2 * dec_width)
    pairs_flops = 2 * rows * width * 2 * dec_width
    own_pairs = call(
        pairs_kernel,
        jax.ShapeDtypeStruct(pairs_shape, jnp.bfloat16),
        "vv",
        "decoder_pairs",
        pairs_flops,
        20,
    )(encoded, got("wk"))
    return call(
        decoder_kernel,
        jax.ShapeDtypeStruct(dec_queries.shape, jnp.float32),
        "svvvv",
        "decoder_attention",
        pairs_flops,
        28,
        scratch=[
            pltpu.VMEM(pairs_shape, jnp.bfloat16),
            pltpu.VMEM((dec_width // HEAD_DIM, dec_queries.shape[0], HEAD_DIM), jnp.float32),
            dma((dec_width // HEAD_DIM,)),
        ],
        out="h",
    )(here, own_pairs, other, got("wk"), dec_queries)


def solution(mesh):
    placed = (
        P("seq", None, "mp"),
        P("seq", "mp"),
        P("seq", None, None),
        P("seq", None),
        P("seq", None),
        P(),
        P(None, "mp"),
        P("mp", None),
        P(),
        P(None, "mp"),
        P("mp", None),
        P(None, None, "mp"),
    )
    return jax.shard_map(
        on_device, mesh=mesh, in_specs=placed, out_specs=P("seq", "mp"), check_vma=False
    )
```
